32 devices in a mesh: graphs: 8 (over z, y), leaves: 4 (over x, core).
Axes of the slice: x: 2, y: 2, z: 4, core: 2. Of those that a mesh axis runs over, the one named last changes fastest.
Arguments:
- centers: float32 [1024, 300], P('graphs'), may hold values from -6 to 6
- leaf_nodes: float32 [1024, 16, 300], P('graphs', 'leaves'), may hold values from -6 to 6
- edges: float32 [1024, 16, 300], P('graphs', 'leaves'), may hold values from -6 to 6
- leaf_counts: int32 [1024], P('graphs'), may hold values from 1 to 16, as said below
- square: float32 [2, 4, 300, 300], replicated, may hold values from -0.375 to 0.375
- out_proj: float32 [2, 300, 300], replicated, may hold values from -1 to 1
- ff_in: float32 [2, 300, 1200], replicated, may hold values from -0.375 to 0.375
- ff_out: float32 [2, 1200, 300], replicated, may hold values from -0.1875 to 0.1875
- ff_bias: float32 [2, 1200], replicated, may hold values from -2 to 2
- biases: float32 [2, 7, 300], replicated, may hold values from -2 to 2
- gains: float32 [2, 2, 300], replicated, may hold values from 0.5 to 1.5
- cot_center: float32 [1024, 300], P('graphs'), may hold values from -6 to 6
- cot_edges: float32 [1024, 16, 300], P('graphs', 'leaves'), may hold values from -6 to 6
Outputs:
- center_out: float32 [1024, 300], P('graphs')
- edges_out: float32 [1024, 16, 300], P('graphs', 'leaves')
- grad_center: float32 [1024, 300], P('graphs')
- grad_leaf_nodes: float32 [1024, 16, 300], P('graphs', 'leaves')
- grad_edges: float32 [1024, 16, 300], P('graphs', 'leaves')
- grad_square: float32 [2, 4, 300, 300], replicated
- grad_out_proj: float32 [2, 300, 300], replicated
- grad_ff_in: float32 [2, 300, 1200], replicated
- grad_ff_out: float32 [2, 1200, 300], replicated
- grad_ff_bias: float32 [2, 1200], replicated
- grad_biases: float32 [2, 7, 300], replicated
- grad_gains: float32 [2, 2, 300], replicated
The draws below stay inside these ranges and needn't reach their ends.
Inputs may be any that keep to these rules, and one draw needn't show every extreme that they name: `leaf_counts`: in every aligned block of 128 graphs one graph has all 16 leaves live.
All inputs are finite; a program needn't handle non-finite values.
Results may differ from the reference program's by a relative error of at most 0.0003.
Values sent between devices are 32-bit elements; how exact they have to be, the bound alone decides.
No kernel may reach another device: no remote copies, remote signals or barrier semaphores. Data moves between devices by JAX's collectives and lax.ppermute only.
A program may use at most 192 MiB of HBM per device.

```python
import jax
import jax.numpy as jnp
from jax import lax

D = 300
HEADS = 12
HEAD_DIM = 25
FF = 1200
LAYERS = 2
GRAPH_DEV = 128
GRAPHS = 1024
SLOTS = 16


def draw_leaf_counts(key, part):
    key = jax.random.fold_in(key, 11)
    key_count, key_place = jax.random.split(key)
    counts = jax.random.randint(key_count, (GRAPHS,), 1, SLOTS + 1)
    blocks = GRAPHS // GRAPH_DEV
    chosen = jax.random.randint(key_place, (blocks, 1), 0, GRAPH_DEV)
    widest = jnp.arange(GRAPH_DEV)[None, :] == chosen
    return jnp.where(widest.reshape(GRAPHS), SLOTS, counts).astype(jnp.int32)


def shard_levels(own_key, shape, shards, smallest, high):
    def one(position, parts):
        steps = jax.random.uniform(jax.random.fold_in(jax.random.fold_in(own_key, 6), position), (parts,), jnp.float32, smallest / len(shards), high / len(shards))
        return jnp.repeat(jnp.exp(steps), shape[position] // parts).reshape((-1,) + (1,) * (len(shape) - position - 1))

    level = one(*shards[0])
    for cut in shards[1:]:
        level = level * one(*cut)
    return level


def gaussian(key, extent, width, limit, shards=(), kind=jnp.bfloat16):
    values = width * jax.random.normal(key, extent, jnp.float32)
    if shards:
        values = values * shard_levels(key, extent, shards, -0.22, 0.18)
    return jnp.clip(values, -limit, limit).astype(kind)


def setup_inputs(seed: int = 0) -> dict:
    seeds = jax.random.split(jax.random.key(seed), 14)
    centers = gaussian(seeds[0], (GRAPHS, D), 1.0, 6.0, ((0, 8),), jnp.float32)
    leaf_nodes = gaussian(seeds[1], (GRAPHS, SLOTS, D), 1.0, 6.0, ((0, 8), (1, 4)), jnp.float32)
    edges = gaussian(seeds[2], (GRAPHS, SLOTS, D), 1.0, 6.0, ((0, 8), (1, 4)), jnp.float32)
    leaf_counts = draw_leaf_counts(jax.random.fold_in(seeds[13], 71), 0)
    square = gaussian(seeds[4], (LAYERS, 4, D, D), D ** -0.5, 0.375, (), jnp.float32)
    out_proj = gaussian(seeds[5], (LAYERS, D, D), (D // 8) ** -0.5, 1.0, (), jnp.float32)
    ff_in = gaussian(seeds[6], (LAYERS, D, FF), D ** -0.5, 0.375, (), jnp.float32)
    ff_out = gaussian(seeds[7], (LAYERS, FF, D), FF ** -0.5, 0.1875, (), jnp.float32)
    ff_bias = gaussian(seeds[8], (LAYERS, FF), 0.3, 2.0, (), jnp.float32)
    biases = gaussian(seeds[9], (LAYERS, 7, D), 0.3, 2.0, (), jnp.float32)
    gains = jnp.clip(1.0 + 0.1 * jax.random.normal(seeds[10], (LAYERS, 2, D), jnp.float32), 0.5, 1.5)
    cot_center = gaussian(seeds[11], (GRAPHS, D), 1.0, 6.0, ((0, 8),), jnp.float32)
    cot_edges = gaussian(seeds[12], (GRAPHS, SLOTS, D), 1.0, 6.0, ((0, 8), (1, 4)), jnp.float32)
    return {"centers": centers, "leaf_nodes": leaf_nodes, "edges": edges, "leaf_counts": leaf_counts, "square": square, "out_proj": out_proj, "ff_in": ff_in, "ff_out": ff_out, "ff_bias": ff_bias, "biases": biases, "gains": gains, "cot_center": cot_center, "cot_edges": cot_edges}


@jax.custom_vjp
def low(v):
    return lax.optimization_barrier(v.astype(jnp.bfloat16)).astype(jnp.float32)

@jax.custom_vjp
def low_back(v):
    return v

def low_keep(v):
    return (low(v), None)

def low_pass(kept, grad):
    return (grad,)

def back_keep(v):
    return (v, None)

def back_low(kept, grad):
    return (low(grad),)
low.defvjp(low_keep, low_pass)
low_back.defvjp(back_keep, back_low)
precise = lax.Precision.HIGHEST

def layer_norm(values, gain, shift):
    centred = values - lax.optimization_barrier(jnp.mean(values, axis=-1, keepdims=True))
    spread = lax.optimization_barrier(jnp.mean(centred * centred, axis=-1, keepdims=True))
    return centred * lax.rsqrt(spread + 1e-05) * gain + shift

def center_block(attended, states, out_weight, in_weight, down_weight, hidden_bias, center_bias, norm_gains):
    projected = jnp.dot(attended, out_weight, precision=precise) + center_bias[1]
    normed_one = layer_norm(states + projected, norm_gains[0], center_bias[2])
    hidden_act = jax.nn.gelu(jnp.dot(normed_one, in_weight, precision=precise) + hidden_bias, approximate=True)
    ff_result = jnp.dot(hidden_act, down_weight, precision=precise) + center_bias[3]
    return layer_norm(normed_one + ff_result, norm_gains[1], center_bias[4])

def carte_layer(states, nodes, edge_rows, live_mask, layer_square, out_weight, in_weight, down_weight, hidden_bias, layer_bias, norm_gains):
    graph_count = states.shape[0]
    messages = nodes * edge_rows
    queries = jnp.dot(states, layer_square[0], precision=precise) + layer_bias[0]
    key_rows = jnp.einsum('gld,de->gle', messages, layer_square[1], precision=precise)
    value_rows = jnp.einsum('gld,de->gle', messages, layer_square[2], precision=precise) + layer_bias[5]
    query_heads = queries.reshape(graph_count, HEADS, HEAD_DIM)
    key_heads = key_rows.reshape(graph_count, SLOTS, HEADS, HEAD_DIM)
    value_heads = value_rows.reshape(graph_count, SLOTS, HEADS, HEAD_DIM)
    scores = jnp.einsum('ghc,glhc->ghl', query_heads, key_heads, precision=precise) * HEAD_DIM ** (-0.5)
    masked = jnp.where(live_mask[:, None, :], scores, -1e+30)
    top_score = lax.optimization_barrier(jnp.max(masked, axis=-1, keepdims=True))
    weights = jnp.where(live_mask[:, None, :], jnp.exp(masked - top_score), 0.0)
    totals = lax.optimization_barrier(jnp.sum(weights, axis=-1))
    attended = jnp.einsum('ghl,glhc->ghc', weights, value_heads, precision=precise) / totals[..., None]
    attended = attended.reshape(graph_count, D)
    new_states = center_block(attended, states, out_weight, in_weight, down_weight, hidden_bias, layer_bias[0:5], norm_gains)
    new_edges = edge_rows + jnp.einsum('gld,de->gle', messages, layer_square[3], precision=precise) + layer_bias[6]
    return (new_states, new_edges)

def reference(centers, leaf_nodes, edges, leaf_counts, square, out_proj, ff_in, ff_out, ff_bias, biases, gains, cot_center, cot_edges):
    live_mask = jnp.arange(SLOTS, dtype=jnp.int32)[None, :] < leaf_counts[:, None]

    def forward(states, nodes, edge_rows, all_square, all_out, all_in, all_down, all_hidden, all_bias, all_gains):
        for layer_at in range(LAYERS):
            states, edge_rows = carte_layer(states, nodes, edge_rows, live_mask, all_square[layer_at], all_out[layer_at], all_in[layer_at], all_down[layer_at], all_hidden[layer_at], all_bias[layer_at], all_gains[layer_at])
        return (states, edge_rows)
    outputs, pullback = jax.vjp(forward, centers, leaf_nodes, edges, square, out_proj, ff_in, ff_out, ff_bias, biases, gains)
    grads = pullback((cot_center, cot_edges))
    return (outputs[0], outputs[1], grads[0], grads[1], grads[2], grads[3], grads[4], grads[5], grads[6], grads[7], grads[8], grads[9])
```

```python
import functools

import jax
import jax.numpy as jnp
from jax import lax
from jax.experimental import pallas as pl
from jax.experimental.pallas import tpu as pltpu
from jax.sharding import PartitionSpec as P

HEADS = 12
HEAD_DIM = 25
LAYERS = 2
LANES = 128
ROWS = 8
HEAD_ROWS = 16
EPS = 1e-05
SCALE = HEAD_DIM ** (-0.5)
GELU_A = 0.7978845608028654
GELU_B = 0.044715

F32 = jnp.float32
BF16 = jnp.bfloat16
NN = (((1,), (0,)), ((), ()))
TN = (((0,), (0,)), ((), ()))
NT = (((1,), (1,)), ((), ()))
BOTH = ("graphs", "leaves")
VMEM = pl.BlockSpec(memory_space=pltpu.VMEM)
SMEM = pl.BlockSpec(memory_space=pltpu.SMEM)


def ceil_div(a, b):
    return -(-a // b)


def dot(a, b, dims):
    return lax.dot_general(a, b, dims, preferred_element_type=F32)


def split(v):
    high = v.astype(BF16)
    return high, (v - high.astype(F32)).astype(BF16)


def mul_pair(a, b, dims):
    return dot(a[0], b[0], dims) + (dot(a[0], b[1], dims) + dot(a[1], b[0], dims))


def mul_narrow(a, b, dims):
    width = b[0].shape[1]
    both = dot(a[0], jnp.concatenate(b, axis=1), dims)
    return both[:, :width] + (both[:, width:] + dot(a[1], b[0], dims))


def outer(a, b):
    left = jnp.concatenate([a[0], a[0], a[1]], axis=1)
    right = jnp.concatenate([b[0], b[1], b[0]], axis=1)
    return dot(left, right, NT)


def lane_sums(v):
    ones = jnp.ones((ROWS, v.shape[1]), BF16)
    high, low = split(v)
    return (dot(ones, high, NT) + dot(ones, low, NT))[0:1, :]


def columns(rows):
    count = rows.shape[0]
    if count % ROWS:
        fill = jnp.zeros((ROWS - count % ROWS, rows.shape[1]), F32)
        rows = jnp.concatenate([rows, fill], axis=0)
    return rows.T


def slot_cols(ref, slots):
    return jnp.concatenate([ref[:, s, :] for s in range(slots)], axis=1)


def leaf_forward(m, square_ref, bias_ref, layer, k_ref, v_ref):
    pair = split(m)
    cols = columns(bias_ref[:, layer, :])
    k_ref[...] = mul_pair(split(square_ref[layer, :, 1, :].T), pair, NN)
    v_ref[...] = mul_pair(split(square_ref[layer, :, 2, :].T), pair, NN) + cols[:, 5:6]
    return mul_pair(split(square_ref[layer, :, 3, :].T), pair, NN) + cols[:, 6:7]


def attend(q_ref, k_ref, v_ref, live, s_ref, w_ref, part_ref):
    slots = len(live)
    s_ref[...] = jnp.zeros(s_ref.shape, F32)
    for h in range(HEADS):
        at = slice(HEAD_DIM * h, HEAD_DIM * (h + 1))
        q = q_ref[at, :]
        for s in range(slots):
            k = k_ref[at, LANES * s : LANES * (s + 1)]
            s_ref[s, h : h + 1, :] = jnp.sum(q * k, axis=0, keepdims=True)
    scores = [jnp.where(live[s], s_ref[s] * SCALE, -1e30) for s in range(slots)]
    top = functools.reduce(jnp.maximum, scores)
    weights = [jnp.where(live[s], jnp.exp(scores[s] - top), 0.0) for s in range(slots)]
    for s in range(slots):
        s_ref[s] = scores[s]
        w_ref[s] = weights[s]
    for h in range(HEADS):
        at = slice(HEAD_DIM * h, HEAD_DIM * (h + 1))
        total = 0.0
        for s in range(slots):
            total += w_ref[s, h : h + 1, :] * v_ref[at, LANES * s : LANES * (s + 1)]
        part_ref[at, :] = total
    width = HEADS * HEAD_DIM
    base = ceil_div(width, ROWS) * ROWS
    part_ref[width:base, :] = jnp.zeros((base - width, LANES), F32)
    part_ref[base : base + HEAD_ROWS, :] = functools.reduce(jnp.add, weights)
    part_ref[base + HEAD_ROWS : base + 2 * HEAD_ROWS, :] = top


def tree(values, op):
    while len(values) > 1:
        values = [op(values[i], values[i + 1]) for i in range(0, len(values), 2)]
    return values[0]


def combine(part_refs, r_ref, att_ref, top_ref, total_ref):
    base = ceil_div(HEADS * HEAD_DIM, ROWS) * ROWS
    totals = [ref[base : base + HEAD_ROWS, :] for ref in part_refs]
    tops = [ref[base + HEAD_ROWS : base + 2 * HEAD_ROWS, :] for ref in part_refs]
    top = tree(tops, jnp.maximum)
    factors = [jnp.exp(t - top) for t in tops]
    total = tree([a * b for a, b in zip(totals, factors)], jnp.add)
    head = lax.broadcasted_iota(jnp.int32, total.shape, 0) < HEADS
    total = jnp.where(head, total, 1.0)
    top_ref[...] = top
    total_ref[...] = total
    for n, factor in enumerate(factors):
        r_ref[n] = factor / total
    for h in range(HEADS):
        at = slice(HEAD_DIM * h, HEAD_DIM * (h + 1))
        att_ref[at, :] = tree(
            [ref[at, :] * r_ref[n, h : h + 1, :] for n, ref in enumerate(part_refs)], jnp.add
        )


def normalise(v):
    centred = v - jnp.mean(v, axis=0, keepdims=True)
    spread = lax.rsqrt(jnp.mean(centred * centred, axis=0, keepdims=True) + EPS)
    return centred * spread, spread


def normalise_back(grad, gain, unit, spread):
    g = grad * gain
    return spread * (
        g - jnp.mean(g, axis=0, keepdims=True) - unit * jnp.mean(g * unit, axis=0, keepdims=True)
    )


def gelu_tanh(z):
    return jnp.tanh(GELU_A * (z + GELU_B * (z * z * z)))


def gelu(z, t):
    return 0.5 * z * (1.0 + t)


def gelu_slope(z, t):
    return 0.5 * (1.0 + t) + 0.5 * z * (1.0 - t * t) * (GELU_A * (1.0 + 3.0 * GELU_B * (z * z)))


def center_forward(att, states, out_ref, in_ref, down_ref, hid_ref, bias_ref, gain_ref, layer):
    cols = columns(bias_ref[:, layer, :])
    gains = columns(gain_ref[layer, :, :])
    hid = columns(hid_ref[layer : layer + 1, :])
    o = mul_narrow(split(out_ref[:, layer, :].T), split(att), NN) + cols[:, 1:2]
    unit1, spread1 = normalise(states + o)
    h1 = unit1 * gains[:, 0:1] + cols[:, 2:3]
    z = mul_narrow(split(in_ref[:, layer, :].T), split(h1), NN) + hid[:, 0:1]
    u = gelu(z, gelu_tanh(z))
    f = mul_narrow(split(down_ref[:, layer, :]), split(u), NN) + cols[:, 3:4]
    unit2, spread2 = normalise(h1 + f)
    return unit1, spread1, z, unit2, spread2, unit2 * gains[:, 1:2] + cols[:, 4:5]


def extend(ref, value):
    rows, width = ref.shape[0], value.shape[0]
    ref[width:rows, :] = jnp.where(
        lax.broadcasted_iota(jnp.int32, (rows - width, value.shape[1]), 0) == 0, 1.0, 0.0
    )
    ref[0:width, :] = value


class Plan:
    def __init__(self, width, hidden, graph_devices, leaf_devices):
        self.width, self.hidden = width, hidden
        self.graph_devices, self.leaf_devices = graph_devices, leaf_devices
        self.row_tiles = ceil_div(width + 4, ROWS)
        self.share = ceil_div(self.row_tiles, leaf_devices)
        self.share_rows = self.share * ROWS
        self.hid_full, self.hid_tail = divmod(hidden, LANES)
        self.wid_full, self.wid_tail = divmod(width, LANES)
        self.center_lanes = 2 * self.hid_full + 1 + self.wid_full + 1
        self.center_tiles = ceil_div(self.share * self.center_lanes, graph_devices)
        self.query_lanes = self.wid_full + 1
        self.query_tiles = ceil_div(self.share * self.query_lanes, graph_devices)
        self.leaf_lanes = 3 * self.wid_full + 2
        self.leaf_tiles = ceil_div(self.row_tiles * self.leaf_lanes, graph_devices * leaf_devices)
        self.chunk_tiles = self.center_tiles + self.query_tiles + self.leaf_tiles
        self.last_owner, self.last_tile = divmod(width // ROWS, self.share)
        self.last_row = width % ROWS


def joint_tail(left, right, width):
    lane = lax.broadcasted_iota(jnp.int32, left.shape, 1)
    return jnp.where(lane < width, left, pltpu.roll(right, width, 1))


def deal(tiles, per_chunk, abs_ref):
    for t, tile in enumerate(tiles):
        chunk, at = divmod(t, per_chunk)
        abs_ref[chunk, at * ROWS : (at + 1) * ROWS, :] = tile
    for t in range(len(tiles), per_chunk * abs_ref.shape[0]):
        chunk, at = divmod(t, per_chunk)
        abs_ref[chunk, at * ROWS : (at + 1) * ROWS, :] = jnp.zeros((ROWS, LANES), F32)


def send_graphs(abs_ref, me, keep_ref, give_ref):
    half = keep_ref.shape[0]
    for r in range(half):
        keep_ref[r] = abs_ref[jnp.bitwise_xor(2 * r, me)]
        give_ref[r] = abs_ref[jnp.bitwise_xor(2 * r + 1, me)]


def center_backward(
    plan, grad, att, states, z, unit1, spread1, unit2, spread2,
    out_ref, in_ref, down_ref, bias_ref, gain_ref, layer, me_graph, me_leaf,
    ext_ref, wide1_ref, wide2_ref, abs_ref, keep_ref, give_ref,
):
    cols = columns(bias_ref[:, layer, :])
    gains = columns(gain_ref[layer, :, :])
    share = pl.ds(pl.multiple_of(me_leaf * plan.share_rows, ROWS), plan.share_rows)
    width, hidden = plan.width, plan.hidden

    g_f = normalise_back(grad, gains[:, 1:2], unit2, spread2)
    t = gelu_tanh(z)
    u = gelu(z, t)
    pair_f = split(g_f)
    dz = mul_narrow(split(down_ref[:, layer, :].T), pair_f, NN) * gelu_slope(z, t)
    pair_z = split(dz)
    g_h1 = g_f + mul_narrow(split(in_ref[:, layer, :]), pair_z, NN)
    g_o = normalise_back(g_h1, gains[:, 0:1], unit1, spread1)
    pair_o = split(g_o)
    g_att = mul_narrow(split(out_ref[:, layer, :]), pair_o, NN)

    extend(ext_ref, unit1 * gains[:, 0:1] + cols[:, 2:3])
    wide1_ref[:, 0:hidden] = outer(split(ext_ref[share, :]), pair_z)
    extend(ext_ref, g_f)
    wide2_ref[:, 0:hidden] = outer(split(ext_ref[share, :]), split(u))
    extend(ext_ref, att)
    own_out = outer(split(ext_ref[share, :]), pair_o)

    sums = [lane_sums(v) for v in (g_h1, g_h1 * unit1, g_f, grad, grad * unit2)]
    row = plan.last_tile * ROWS + plan.last_row

    @pl.when(me_leaf == plan.last_owner)
    def _():
        wide2_ref[row + 1 : row + 2, 0:width] = sums[3]
        wide2_ref[row + 2 : row + 3, 0:width] = sums[4]

    tiles = []
    for r in range(plan.share):
        at = slice(r * ROWS, (r + 1) * ROWS)
        for ref in (wide1_ref, wide2_ref):
            tiles += [ref[at, LANES * c : LANES * (c + 1)] for c in range(plan.hid_full)]
        tail = slice(LANES * plan.hid_full, LANES * (plan.hid_full + 1))
        tiles.append(joint_tail(wide1_ref[at, tail], wide2_ref[at, tail], plan.hid_tail))
        for c in range(plan.wid_full + 1):
            tiles.append((r, c))
    wide1_ref[:, 0:width] = own_out

    @pl.when(me_leaf == plan.last_owner)
    def _():
        for n in range(3):
            wide1_ref[row + 1 + n : row + 2 + n, 0:width] = sums[n]

    tiles = [
        wide1_ref[t[0] * ROWS : (t[0] + 1) * ROWS, LANES * t[1] : LANES * (t[1] + 1)]
        if isinstance(t, tuple)
        else t
        for t in tiles
    ]
    deal(tiles, plan.center_tiles, abs_ref)
    send_graphs(abs_ref, me_graph, keep_ref, give_ref)
    return g_att, g_o


def attend_back(att_ref, gatt_ref, q_ref, k_ref, v_ref, s_ref, top, total, slots, ct_ref, p_ref, gq_ref, gk_ref, gv_ref):
    for s in range(slots):
        p_ref[s] = jnp.exp(s_ref[s] - top) / total
    for h in range(HEADS):
        at = slice(HEAD_DIM * h, HEAD_DIM * (h + 1))
        ga, q = gatt_ref[at, :], q_ref[at, :]
        centre = jnp.sum(ga * att_ref[at, :], axis=0, keepdims=True)
        gq = 0.0
        for s in range(slots):
            lanes = slice(LANES * s, LANES * (s + 1))
            k = k_ref[at, lanes]
            p = p_ref[s, h : h + 1, :]
            gp = jnp.sum(ga * v_ref[at, lanes], axis=0, keepdims=True)
            gs = p * (gp - centre) * SCALE
            gv_ref[at, lanes] = p * ga
            gk_ref[at, lanes] = gs * q
            gq += gs * k
        gq_ref[at, :] = gq


def query_gradient(plan, states, gq, me_graph, me_leaf, ext_ref, wide_ref, abs_ref, keep_ref, give_ref):
    share = pl.ds(pl.multiple_of(me_leaf * plan.share_rows, ROWS), plan.share_rows)
    extend(ext_ref, states)
    wide_ref[:, 0 : plan.width] = outer(split(ext_ref[share, :]), split(gq))
    tiles = [
        wide_ref[r * ROWS : (r + 1) * ROWS, LANES * c : LANES * (c + 1)]
        for r in range(plan.share)
        for c in range(plan.query_lanes)
    ]
    deal(tiles, plan.query_tiles, abs_ref)
    send_graphs(abs_ref, me_graph, keep_ref, give_ref)


def live_rows(me_ref, count_ref, slots):
    first = me_ref[1] * slots
    return [count_ref[...] > first + s for s in range(slots)]


def first_kernel(slots, me_ref, count_ref, x_ref, e_ref, h_ref, square_ref, bias_ref,
                 part_ref, q_ref, k_ref, v_ref, s_ref, e1_ref, w_ref):
    cols = columns(bias_ref[:, 0, :])
    m = slot_cols(x_ref, slots) * slot_cols(e_ref, slots)
    q_ref[...] = mul_narrow(split(square_ref[0, :, 0, :].T), split(h_ref[...]), NN) + cols[:, 0:1]
    step = leaf_forward(m, square_ref, bias_ref, 0, k_ref, v_ref)
    for s in range(slots):
        e1_ref[:, s, :] = e_ref[:, s, :] + step[:, LANES * s : LANES * (s + 1)]
    attend(q_ref, k_ref, v_ref, live_rows(me_ref, count_ref, slots), s_ref, w_ref, part_ref)


def second_kernel(slots, x_ref, e1_ref, square_ref, bias_ref, k_ref, v_ref, e2_ref):
    m = slot_cols(x_ref, slots) * slot_cols(e1_ref, slots)
    step = leaf_forward(m, square_ref, bias_ref, 1, k_ref, v_ref)
    for s in range(slots):
        e2_ref[:, s, :] = e1_ref[:, s, :] + step[:, LANES * s : LANES * (s + 1)]


def third_kernel(slots, me_ref, count_ref, p0, p1, p2, p3, h_ref, k_ref, v_ref, square_ref, out_ref, in_ref, down_ref,
                 hid_ref, bias_ref, gain_ref,
                 part_ref, att_ref, top_ref, total_ref, unit1_ref, spread1_ref, z_ref, unit2_ref, spread2_ref, h2_ref,
                 q_ref, s_ref, r_ref, w_ref):
    combine([p0, p1, p2, p3], r_ref, att_ref, top_ref, total_ref)
    unit1, spread1, z, unit2, spread2, h2 = center_forward(
        att_ref[...], h_ref[...], out_ref, in_ref, down_ref, hid_ref, bias_ref, gain_ref, 0
    )
    unit1_ref[...] = unit1
    spread1_ref[...] = spread1
    z_ref[...] = z
    unit2_ref[...] = unit2
    spread2_ref[...] = spread2
    h2_ref[...] = h2
    cols = columns(bias_ref[:, 1, :])
    q_ref[...] = mul_narrow(split(square_ref[1, :, 0, :].T), split(h2), NN) + cols[:, 0:1]
    attend(q_ref, k_ref, v_ref, live_rows(me_ref, count_ref, slots), s_ref, w_ref, part_ref)


def fourth_kernel(plan, slots, me_ref, p0, p1, p2, p3, h_ref, q_ref, k_ref, v_ref, s_ref, cot_ref, out_ref, in_ref,
                  down_ref, hid_ref, bias_ref, gain_ref,
                  center_ref, gq_ref, gk_ref, gv_ref, res_ref, keep_ref, give_ref,
                  r_ref, att_ref, top_ref, total_ref, gatt_ref, p_ref, ext_ref, wide1_ref, wide2_ref, abs_ref):
    combine([p0, p1, p2, p3], r_ref, att_ref, top_ref, total_ref)
    unit1, spread1, z, unit2, spread2, out = center_forward(
        att_ref[...], h_ref[...], out_ref, in_ref, down_ref, hid_ref, bias_ref, gain_ref, 1
    )
    center_ref[...] = out
    gatt_ref[...], res_ref[...] = center_backward(
        plan, cot_ref[...], att_ref[...], h_ref[...], z, unit1, spread1, unit2, spread2,
        out_ref, in_ref, down_ref, bias_ref, gain_ref, 1, me_ref[0], me_ref[1],
        ext_ref, wide1_ref, wide2_ref, abs_ref, keep_ref, give_ref,
    )
    attend_back(att_ref, gatt_ref, q_ref, k_ref, v_ref, s_ref, top_ref[...], total_ref[...], slots,
                None, p_ref, gq_ref, gk_ref, gv_ref)


def fifth_kernel(plan, slots, layer, last, me_ref, x_ref, e_ref, ge_ref, *refs):
    if last:
        gx_ref, *refs = refs
    (gk_ref, gv_ref, square_ref, new_gx_ref, new_ge_ref, core_ref, give_ref, keep_ref, ext_ref, wide_ref, abs_ref) = refs
    extend(ext_ref, slot_cols(x_ref, slots) * slot_cols(e_ref, slots))
    ge = slot_cols(ge_ref, slots)
    pairs = [split(v) for v in (gk_ref[...], gv_ref[...], ge)]
    gm = tree([mul_pair(split(square_ref[layer, :, n + 1, :]), pairs[n], NN) for n in range(2)], jnp.add)
    gm = gm + mul_pair(split(square_ref[layer, :, 3, :]), pairs[2], NN)
    for s in range(slots):
        part = gm[:, LANES * s : LANES * (s + 1)]
        gx = part * e_ref[:, s, :]
        new_gx_ref[:, s, :] = gx_ref[:, s, :] + gx if last else gx
        new_ge_ref[:, s, :] = ge_ref[:, s, :] + part * x_ref[:, s, :]
    m = split(ext_ref[...])
    for n in range(3):
        wide_ref[n, :, 0 : plan.width] = outer(m, pairs[n])
    tiles = []
    for r in range(plan.row_tiles):
        at = slice(r * ROWS, (r + 1) * ROWS)
        for n in range(3):
            tiles += [wide_ref[n, at, LANES * c : LANES * (c + 1)] for c in range(plan.wid_full)]
        tail = slice(LANES * plan.wid_full, LANES * (plan.wid_full + 1))
        tiles.append(joint_tail(wide_ref[0, at, tail], wide_ref[1, at, tail], plan.wid_tail))
        tiles.append(wide_ref[2, at, tail])
    deal(tiles, plan.leaf_tiles, abs_ref)
    me_graph, me_leaf = me_ref[0], me_ref[1]
    half = plan.graph_devices // 2
    for other in range(plan.leaf_devices):
        leaf = jnp.bitwise_xor(other, me_leaf)
        for r in range(plan.graph_devices):
            rel = 2 * (r % half) + r // half
            source = abs_ref[jnp.bitwise_xor(rel, me_graph) * plan.leaf_devices + leaf]
            if other % 2:
                core_ref[other // 2, r] = source
            elif other // 2:
                give_ref[r] = source
            else:
                keep_ref[r] = source


def sixth_kernel(plan, slots, me_ref, g0, g1, g2, g3, res_ref, h2_ref, square_ref,
                 att_ref, h_ref, z_ref, unit1_ref, spread1_ref, unit2_ref, spread2_ref, top_ref, total_ref,
                 q_ref, k_ref, v_ref, s_ref, out_ref, in_ref, down_ref, bias_ref, gain_ref,
                 gq_ref, gk_ref, gv_ref, new_res_ref, keep_ref, give_ref, q_keep_ref, q_give_ref,
                 gatt_ref, p_ref, ext_ref, wide1_ref, wide2_ref, abs_ref, q_abs_ref):
    gq = tree([ref[...] for ref in (g0, g1, g2, g3)], jnp.add)
    grad = res_ref[...] + mul_narrow(split(square_ref[1, :, 0, :]), split(gq), NN)
    query_gradient(plan, h2_ref[...], gq, me_ref[0], me_ref[1], ext_ref, wide1_ref, q_abs_ref, q_keep_ref, q_give_ref)
    gatt_ref[...], new_res_ref[...] = center_backward(
        plan, grad, att_ref[...], h_ref[...], z_ref[...], unit1_ref[...], spread1_ref[...], unit2_ref[...],
        spread2_ref[...], out_ref, in_ref, down_ref, bias_ref, gain_ref, 0, me_ref[0], me_ref[1],
        ext_ref, wide1_ref, wide2_ref, abs_ref, keep_ref, give_ref,
    )
    attend_back(att_ref, gatt_ref, q_ref, k_ref, v_ref, s_ref, top_ref[...], total_ref[...], slots,
                None, p_ref, gq_ref, gk_ref, gv_ref)


def seventh_kernel(plan, me_ref, g0, g1, g2, g3, res_ref, h_ref, square_ref,
                   grad_ref, keep_ref, give_ref, ext_ref, wide_ref, abs_ref):
    gq = tree([ref[...] for ref in (g0, g1, g2, g3)], jnp.add)
    grad_ref[...] = res_ref[...] + mul_narrow(split(square_ref[0, :, 0, :]), split(gq), NN)
    query_gradient(plan, h_ref[...], gq, me_ref[0], me_ref[1], ext_ref, wide_ref, abs_ref, keep_ref, give_ref)


def last_kernel(plan, routes, me_ref, *refs):
    pieces = [refs[len(routes) * layer : len(routes) * (layer + 1)] for layer in range(LAYERS)]
    square_ref, out_ref, in_ref, down_ref, hid_ref, bias_ref, gain_ref, all_ref = refs[len(routes) * LAYERS :]
    me_graph, me_leaf = me_ref[0], me_ref[1]
    width, hidden = plan.width, plan.hidden
    for layer in range(LAYERS):
        for ref, (graph_bits, leaf, first, rows) in zip(pieces[layer], routes):
            for n, graph in enumerate(graph_bits):
                all_ref[
                    jnp.bitwise_xor(graph, me_graph), jnp.bitwise_xor(leaf, me_leaf), first : first + rows, :
                ] = ref[n]

        def tile(kind, index):
            per = (plan.center_tiles, plan.query_tiles, plan.leaf_tiles)[kind]
            base = (0, plan.center_tiles, plan.center_tiles + plan.query_tiles)[kind]
            leaf, index = index if kind < 2 else (None, index)
            chunk, at = divmod(index, per)
            if kind == 2:
                chunk, leaf = divmod(chunk, plan.leaf_devices)
            at = (base + at) * ROWS
            return all_ref[chunk, leaf, at : at + ROWS, :]

        hid_tail, wid_tail = plan.hid_tail, plan.wid_tail
        for r in range(plan.row_tiles):
            leaf, own = divmod(r, plan.share)
            rows = min(ROWS, width - r * ROWS)
            at = slice(r * ROWS, r * ROWS + rows)
            center = [tile(0, (leaf, own * plan.center_lanes + c)) for c in range(plan.center_lanes)]
            query = [tile(1, (leaf, own * plan.query_lanes + c)) for c in range(plan.query_lanes)]
            sides = [tile(2, r * plan.leaf_lanes + c) for c in range(plan.leaf_lanes)]
            full, wid = plan.hid_full, plan.wid_full
            tail = center[2 * full]
            ins = center[:full] + [tail]
            downs = center[full : 2 * full] + [pltpu.roll(tail, LANES - hid_tail, 1)]
            outs = center[2 * full + 1 :]
            joint = sides[3 * wid]
            keys = sides[:wid] + [joint]
            values = sides[wid : 2 * wid] + [pltpu.roll(joint, LANES - wid_tail, 1)]
            sides_e = sides[2 * wid : 3 * wid] + [sides[3 * wid + 1]]
            for c in range(full + 1):
                count = LANES if c < full else hid_tail
                lanes = slice(LANES * c, LANES * c + count)
                in_ref[at, layer, lanes] = ins[c][:rows, :count]
                down_ref[at, layer, lanes] = downs[c][:rows, :count]
            for c in range(wid + 1):
                count = LANES if c < wid else wid_tail
                lanes = slice(LANES * c, LANES * c + count)
                out_ref[at, layer, lanes] = outs[c][:rows, :count]
                for n, part in enumerate((query, keys, values, sides_e)):
                    square_ref[layer, at, n, lanes] = part[c][:rows, :count]
            if r == width // ROWS:
                first = plan.last_row
                for c in range(full + 1):
                    count = LANES if c < full else hid_tail
                    lanes = slice(LANES * c, LANES * c + count)
                    hid_ref[layer : layer + 1, lanes] = ins[c][first : first + 1, :count]
                for c in range(wid + 1):
                    count = LANES if c < wid else wid_tail
                    lanes = slice(LANES * c, LANES * c + count)
                    found = (
                        (query, 0), (outs, 0), (outs, 1), (outs, 3), (downs, 1), (values, 0), (sides_e, 0),
                    )
                    for n, (part, row) in enumerate(found):
                        bias_ref[n, layer : layer + 1, lanes] = part[c][first + row : first + row + 1, :count]
                    gain_ref[layer, 0:1, lanes] = outs[c][first + 2 : first + 3, :count]
                    gain_ref[layer, 1:2, lanes] = downs[c][first + 2 : first + 3, :count]


def swap(values, axis, size, distance):
    pairs = [(i, i ^ distance) for i in range(size)]
    return jax.tree.map(lambda v: lax.ppermute(v, axis, pairs), values)


def bit_groups(size):
    bits, groups = size.bit_length() - 1, []
    at = bits
    while at > 1:
        low = max(1, at - 2)
        groups.append((low, at - low))
        at = low
    return groups


def graph_scatter(keep, give, size):
    got = swap(give, "graphs", size, 1)
    held = [keep, got]
    half = size // 2
    for low, count in bit_groups(size):
        ways = 1 << count
        step = half // ways
        parts = [tree([v[step * k : step * (k + 1)] for v in held], jnp.add) if len(held) in (1, 2, 4) else None for k in range(ways)]
        held = [parts[0]] + [swap(parts[k], "graphs", size, k << low) for k in range(1, ways)]
        half = step
    return tree(held, jnp.add)[0]


def leaf_scatter(core, give, keep, sizes):
    got = swap(core, "leaves", sizes[1], 1)
    far = swap(give + got[1], "leaves", sizes[1], 2)
    half = sizes[0] // 2
    even = (keep[:half] + got[0, :half]) + far[:half]
    odd = (keep[half:] + got[0, half:]) + far[half:]
    return graph_scatter(even, odd, sizes[0])


def gather(chunk, sizes):
    graph_devices, leaf_devices = sizes
    held = [chunk]
    graphs = [0]
    for low, count in reversed(bit_groups(graph_devices)):
        ways = 1 << count
        held = held + [swap(v, "graphs", graph_devices, k << low) for k in range(1, ways) for v in held]
        graphs = graphs + [g ^ (k << low) for k in range(1, ways) for g in graphs]
    rows = chunk.shape[0]
    middle = rows // 2 // ROWS * ROWS
    pieces, routes = [], []
    for n, (first, last) in enumerate(((0, middle), (middle, rows))):
        block = jnp.stack([v[first:last] for v in held])
        parts = [(block, 0, 0)]
        for turn in (0, 1) if n else (1, 0):
            if turn:
                parts = parts + [(swap(v, "graphs", graph_devices, 1), g ^ 1, f) for v, g, f in parts]
            else:
                parts = parts + [(swap(v, "leaves", leaf_devices, 2), g, f ^ 2) for v, g, f in parts]
        parts = parts + [(swap(v, "leaves", leaf_devices, 1), g, f ^ 1) for v, g, f in parts]
        pieces += [v for v, _, _ in parts]
        routes += [(tuple(x ^ g for x in graphs), f, first, last - first) for _, g, f in parts]
    return pieces, routes


def on_device(
    sizes,
    centers,
    leaf_nodes,
    edges,
    leaf_counts,
    square,
    out_proj,
    ff_in,
    ff_out,
    ff_bias,
    biases,
    gains,
    cot_center,
    cot_edges,
):
    graphs, slots, width = leaf_nodes.shape
    hidden = ff_in.shape[2]
    graph_devices, leaf_devices = sizes
    plan = Plan(width, hidden, graph_devices, leaf_devices)
    me = jnp.stack([lax.axis_index("graphs"), lax.axis_index("leaves")]).astype(jnp.int32)

    h = centers.T
    x = leaf_nodes.transpose(2, 1, 0)
    e = edges.transpose(2, 1, 0)
    count = leaf_counts.reshape(1, graphs)
    sq = square.transpose(0, 2, 1, 3)
    wo = out_proj.transpose(1, 0, 2)
    w1 = ff_in.transpose(1, 0, 2)
    w2 = ff_out.transpose(2, 0, 1)
    bias = biases.transpose(1, 0, 2)
    gc = cot_center.T
    ge = cot_edges.transpose(2, 1, 0)

    base = ceil_div(width, ROWS) * ROWS
    wide = plan.share_rows
    lanes = ceil_div(hidden, LANES) * LANES
    shape = lambda *s: jax.ShapeDtypeStruct(s, F32)
    scratch = lambda *s: pltpu.VMEM(s, F32)
    cell = (width, graphs)
    row = (1, graphs)
    sides = (width, slots * graphs)
    cube = (width, slots, graphs)
    heads = (HEAD_ROWS, graphs)
    scores = (slots, HEAD_ROWS, graphs)
    part = (base + 2 * HEAD_ROWS, graphs)
    half = graph_devices // 2

    def call(kernel, ins, outs, scratches, first_smem=True, flops=0):
        return pl.pallas_call(
            kernel,
            in_specs=[SMEM if first_smem and n == 0 else VMEM for n in range(len(ins))],
            out_specs=[VMEM] * len(outs),
            out_shape=[shape(*s) for s in outs],
            scratch_shapes=[scratch(*s) for s in scratches],
            compiler_params=pltpu.CompilerParams(vmem_limit_bytes=56 << 20),
            cost_estimate=pl.CostEstimate(flops=flops, bytes_accessed=0, transcendentals=0),
        )(*ins)

    def around(value):
        return [value] + [swap(value, "leaves", leaf_devices, k) for k in range(1, leaf_devices)]

    part1, q1, k1, v1, s1, e1 = call(
        functools.partial(first_kernel, slots),
        (me, count, x, e, h, sq, bias),
        (part, cell, sides, sides, scores, cube),
        (scores,),
    )
    parts1 = around(part1)
    k2, v2, e2 = call(
        functools.partial(second_kernel, slots), (x, e1, sq, bias), (sides, sides, cube), (), first_smem=False
    )
    part2, att1, top1, total1, unit1, spread1, z1, unit2, spread2, h2, q2, s2 = call(
        functools.partial(third_kernel, slots),
        (me, count, *parts1, h, k2, v2, sq, wo, w1, w2, ff_bias, bias, gains),
        (part, cell, heads, heads, cell, row, (hidden, graphs), cell, row, cell, cell, scores),
        ((leaf_devices, *heads), scores),
    )
    parts2 = around(part2)
    center_chunk = (half, plan.center_tiles * ROWS, LANES)
    query_chunk = (half, plan.query_tiles * ROWS, LANES)
    leaf_chunk = (graph_devices, plan.leaf_tiles * ROWS, LANES)
    ext = (wide * leaf_devices, graphs)
    center_out, gq2, gk2, gv2, res2, keep2, give2 = call(
        functools.partial(fourth_kernel, plan, slots),
        (me, *parts2, h2, q2, k2, v2, s2, gc, wo, w1, w2, ff_bias, bias, gains),
        (cell, cell, sides, sides, cell, center_chunk, center_chunk),
        ((leaf_devices, *heads), cell, heads, heads, cell, scores, ext, (wide, lanes), (wide, lanes),
         (graph_devices, *center_chunk[1:])),
    )
    gqs2 = around(gq2)
    leaf_scratch = (
        (plan.row_tiles * ROWS, slots * graphs),
        (3, plan.row_tiles * ROWS, ceil_div(width, LANES) * LANES),
        (graph_devices * leaf_devices, *leaf_chunk[1:]),
    )
    gx2, ge1, lcore2, lgive2, lkeep2 = call(
        functools.partial(fifth_kernel, plan, slots, 1, False),
        (me, x, e1, ge, gk2, gv2, sq),
        (cube, cube, (2, *leaf_chunk), leaf_chunk, leaf_chunk),
        leaf_scratch,
    )
    gq1, gk1, gv1, res1, keep1, give1, qkeep2, qgive2 = call(
        functools.partial(sixth_kernel, plan, slots),
        (me, *gqs2, res2, h2, sq, att1, h, z1, unit1, spread1, unit2, spread2, top1, total1,
         q1, k1, v1, s1, wo, w1, w2, bias, gains),
        (cell, sides, sides, cell, center_chunk, center_chunk, query_chunk, query_chunk),
        (cell, scores, ext, (wide, lanes), (wide, lanes),
         (graph_devices, *center_chunk[1:]), (graph_devices, *query_chunk[1:])),
    )
    gqs1 = around(gq1)
    gx1, ge0, lcore1, lgive1, lkeep1 = call(
        functools.partial(fifth_kernel, plan, slots, 0, True),
        (me, x, e, ge1, gx2, gk1, gv1, sq),
        (cube, cube, (2, *leaf_chunk), leaf_chunk, leaf_chunk),
        leaf_scratch,
    )
    grad_center, qkeep1, qgive1 = call(
        functools.partial(seventh_kernel, plan),
        (me, *gqs1, res1, h, sq),
        (cell, query_chunk, query_chunk),
        (ext, (wide, lanes), (graph_devices, *query_chunk[1:])),
    )

    def reduced(keep, give, q_keep, q_give, core, l_give, l_keep):
        return jnp.concatenate(
            [
                graph_scatter(keep, give, graph_devices),
                graph_scatter(q_keep, q_give, graph_devices),
                leaf_scatter(core, l_give, l_keep, sizes),
            ],
            axis=0,
        )

    chunks2 = reduced(keep2, give2, qkeep2, qgive2, lcore2, lgive2, lkeep2)
    chunks1 = reduced(keep1, give1, qkeep1, qgive1, lcore1, lgive1, lkeep1)
    pieces2, routes = gather(chunks2, sizes)
    pieces1, _ = gather(chunks1, sizes)
    g_square, g_out, g_in, g_down, g_hid, g_bias, g_gain = call(
        functools.partial(last_kernel, plan, routes),
        (me, *pieces1, *pieces2),
        ((LAYERS, width, 4, width), (width, LAYERS, width), (width, LAYERS, hidden), (width, LAYERS, hidden),
         (LAYERS, hidden), (7, LAYERS, width), (LAYERS, 2, width)),
        ((graph_devices, leaf_devices, plan.chunk_tiles * ROWS, LANES),),
    )
    return (
        center_out.T,
        e2.transpose(2, 1, 0),
        grad_center.T,
        gx1.transpose(2, 1, 0),
        ge0.transpose(2, 1, 0),
        g_square.transpose(0, 2, 1, 3),
        g_out.transpose(1, 0, 2),
        g_in.transpose(1, 0, 2),
        g_down.transpose(1, 2, 0),
        g_hid,
        g_bias.transpose(1, 0, 2),
        g_gain,
    )


def solution(mesh):
    sizes = (mesh.shape["graphs"], mesh.shape["leaves"])
    in_specs = (
        P("graphs", None),
        P("graphs", "leaves", None),
        P("graphs", "leaves", None),
        P("graphs"),
        P(),
        P(),
        P(),
        P(),
        P(),
        P(),
        P(),
        P("graphs", None),
        P("graphs", "leaves", None),
    )
    out_specs = (
        P("graphs", None),
        P("graphs", "leaves", None),
        P("graphs", None),
        P("graphs", "leaves", None),
        P("graphs", "leaves", None),
        P(),
        P(),
        P(),
        P(),
        P(),
        P(),
        P(),
    )
    return jax.shard_map(
        functools.partial(on_device, sizes),
        mesh=mesh,
        in_specs=in_specs,
        out_specs=out_specs,
        check_vma=False,
    )
```

```python
import functools

import jax
import jax.numpy as jnp
from jax import lax
from jax.experimental import pallas as pl
from jax.experimental.pallas import tpu as pltpu
from jax.sharding import PartitionSpec as P

HEADS = 12
HEAD_DIM = 25
LAYERS = 2
LANES = 128
ROWS = 8
HEAD_ROWS = 16
EPS = 1e-05
KERNEL_VMEM = 24 << 20
LAST_VMEM = 28 << 20
FLOPS_A_US = 5e9
SCALE = HEAD_DIM ** (-0.5)
GELU_A = 0.7978845608028654
GELU_B = 0.044715

F32 = jnp.float32
BF16 = jnp.bfloat16
NN = (((1,), (0,)), ((), ()))
TN = (((0,), (0,)), ((), ()))
NT = (((1,), (1,)), ((), ()))
BOTH = ("graphs", "leaves")
VMEM = pl.BlockSpec(memory_space=pltpu.VMEM)
SMEM = pl.BlockSpec(memory_space=pltpu.SMEM)
HBM = pl.BlockSpec(memory_space=pltpu.HBM)


def ceil_div(a, b):
    return -(-a // b)


def dot(a, b, dims):
    return lax.dot_general(a, b, dims, preferred_element_type=F32)


def split(v):
    high = v.astype(BF16)
    return high, (v - high.astype(F32)).astype(BF16)


def mul_pair(a, b, dims):
    return dot(a[0], b[0], dims) + (dot(a[0], b[1], dims) + dot(a[1], b[0], dims))


def mul_narrow(a, b, dims):
    width = b[0].shape[1]
    both = dot(a[0], jnp.concatenate(b, axis=1), dims)
    return both[:, :width] + (both[:, width:] + dot(a[1], b[0], dims))


def outer(a, b):
    left = jnp.concatenate([a[0], a[0], a[1]], axis=1)
    right = jnp.concatenate([b[0], b[1], b[0]], axis=1)
    return dot(left, right, NT)


def lane_sums(v):
    ones = jnp.ones((ROWS, v.shape[1]), BF16)
    high, low = split(v)
    return (dot(ones, high, NT) + dot(ones, low, NT))[0:1, :]


def columns(rows):
    count = rows.shape[0]
    if count % ROWS:
        fill = jnp.zeros((ROWS - count % ROWS, rows.shape[1]), F32)
        rows = jnp.concatenate([rows, fill], axis=0)
    return rows.T


def plain(value, ref):
    rows, lanes = value.shape
    ref[0:rows, 0:lanes] = value
    return ref[0:rows, 0:lanes]


def slot_cols(ref, slots):
    return jnp.concatenate([ref[:, s, :] for s in range(slots)], axis=1)


def leaf_forward(m, square_ref, bias_ref, layer, k_ref, v_ref):
    pair = split(m)
    cols = columns(bias_ref[:, layer, :])
    k_ref[...] = mul_pair(split(square_ref[layer, :, 1, :].T), pair, NN)
    v_ref[...] = mul_pair(split(square_ref[layer, :, 2, :].T), pair, NN) + cols[:, 5:6]
    return mul_pair(split(square_ref[layer, :, 3, :].T), pair, NN) + cols[:, 6:7]


def attend(q_ref, k_ref, v_ref, live, s_ref, w_ref, part_ref):
    slots = len(live)
    s_ref[...] = jnp.zeros(s_ref.shape, F32)
    for h in range(HEADS):
        at = slice(HEAD_DIM * h, HEAD_DIM * (h + 1))
        q = q_ref[at, :]
        for s in range(slots):
            k = k_ref[at, LANES * s : LANES * (s + 1)]
            s_ref[s, h : h + 1, :] = jnp.sum(q * k, axis=0, keepdims=True)
    scores = [jnp.where(live[s], s_ref[s] * SCALE, -1e30) for s in range(slots)]
    top = functools.reduce(jnp.maximum, scores)
    weights = [jnp.where(live[s], jnp.exp(scores[s] - top), 0.0) for s in range(slots)]
    for s in range(slots):
        s_ref[s] = scores[s]
        w_ref[s] = weights[s]
    for h in range(HEADS):
        at = slice(HEAD_DIM * h, HEAD_DIM * (h + 1))
        total = 0.0
        for s in range(slots):
            total += w_ref[s, h : h + 1, :] * v_ref[at, LANES * s : LANES * (s + 1)]
        part_ref[at, :] = total
    width = HEADS * HEAD_DIM
    base = ceil_div(width, ROWS) * ROWS
    part_ref[width:base, :] = jnp.zeros((base - width, LANES), F32)
    part_ref[base : base + HEAD_ROWS, :] = functools.reduce(jnp.add, weights)
    part_ref[base + HEAD_ROWS : base + 2 * HEAD_ROWS, :] = top


def tree(values, op):
    while len(values) > 1:
        values = [op(values[i], values[i + 1]) for i in range(0, len(values), 2)]
    return values[0]


def combine(part_refs, r_ref, att_ref, top_ref, total_ref):
    base = ceil_div(HEADS * HEAD_DIM, ROWS) * ROWS
    totals = [ref[base : base + HEAD_ROWS, :] for ref in part_refs]
    tops = [ref[base + HEAD_ROWS : base + 2 * HEAD_ROWS, :] for ref in part_refs]
    top = tree(tops, jnp.maximum)
    factors = [jnp.exp(t - top) for t in tops]
    total = tree([a * b for a, b in zip(totals, factors)], jnp.add)
    head = lax.broadcasted_iota(jnp.int32, total.shape, 0) < HEADS
    total = jnp.where(head, total, 1.0)
    top_ref[...] = top
    total_ref[...] = total
    for n, factor in enumerate(factors):
        r_ref[n] = factor / total
    for h in range(HEADS):
        at = slice(HEAD_DIM * h, HEAD_DIM * (h + 1))
        att_ref[at, :] = tree(
            [ref[at, :] * r_ref[n, h : h + 1, :] for n, ref in enumerate(part_refs)], jnp.add
        )


def normalise(v):
    centred = v - jnp.mean(v, axis=0, keepdims=True)
    spread = lax.rsqrt(jnp.mean(centred * centred, axis=0, keepdims=True) + EPS)
    return centred * spread, spread


def normalise_back(grad, gain, unit, spread):
    g = grad * gain
    return spread * (
        g - jnp.mean(g, axis=0, keepdims=True) - unit * jnp.mean(g * unit, axis=0, keepdims=True)
    )


def gelu_tanh(z):
    return jnp.tanh(GELU_A * (z + GELU_B * (z * z * z)))


def gelu(z, t):
    return 0.5 * z * (1.0 + t)


def gelu_slope(z, t):
    return 0.5 * (1.0 + t) + 0.5 * z * (1.0 - t * t) * (GELU_A * (1.0 + 3.0 * GELU_B * (z * z)))


def center_forward(att, states, out_ref, in_ref, down_ref, hid_ref, bias_ref, gain_ref, layer, flat_ref):
    cols = columns(bias_ref[:, layer, :])
    gains = columns(gain_ref[layer, :, :])
    hid = columns(hid_ref[layer : layer + 1, :])
    o = mul_narrow(split(out_ref[:, layer, :].T), split(att), NN) + cols[:, 1:2]
    unit1, spread1 = normalise(states + o)
    h1 = unit1 * gains[:, 0:1] + cols[:, 2:3]
    z = mul_narrow(split(in_ref[:, layer, :].T), split(h1), NN) + hid[:, 0:1]
    u = gelu(z, gelu_tanh(z))
    f = mul_narrow(split(plain(down_ref[:, layer, :], flat_ref)), split(u), NN) + cols[:, 3:4]
    unit2, spread2 = normalise(h1 + f)
    return unit1, spread1, z, unit2, spread2, unit2 * gains[:, 1:2] + cols[:, 4:5]


def extend(ref, value):
    rows, width = ref.shape[0], value.shape[0]
    ref[width:rows, :] = jnp.where(
        lax.broadcasted_iota(jnp.int32, (rows - width, value.shape[1]), 0) == 0, 1.0, 0.0
    )
    ref[0:width, :] = value


class Plan:
    def __init__(self, width, hidden, graph_devices, leaf_devices):
        self.width, self.hidden = width, hidden
        self.graph_devices, self.leaf_devices = graph_devices, leaf_devices
        self.row_tiles = ceil_div(width + 4, ROWS)
        self.share = ceil_div(self.row_tiles, leaf_devices)
        self.share_rows = self.share * ROWS
        self.hid_full, self.hid_tail = divmod(hidden, LANES)
        self.wid_full, self.wid_tail = divmod(width, LANES)
        self.center_lanes = 2 * self.hid_full + 1 + self.wid_full + 1
        self.center_tiles = ceil_div(self.share * self.center_lanes, graph_devices)
        self.query_lanes = self.wid_full + 1
        self.query_tiles = ceil_div(self.share * self.query_lanes, graph_devices)
        self.leaf_lanes = 3 * self.wid_full + 2
        self.leaf_tiles = ceil_div(self.row_tiles * self.leaf_lanes, graph_devices * leaf_devices)
        self.side_tiles = self.query_tiles + self.leaf_tiles
        self.all_tiles = 2 * (self.center_tiles + self.side_tiles)
        side = (2 * self.center_tiles + self.side_tiles, 2 * self.center_tiles)
        self.bases = [
            (self.center_tiles if layer == 0 else 0, side[layer], side[layer] + self.query_tiles) for layer in (0, 1)
        ]
        self.last_owner, self.last_tile = divmod(width // ROWS, self.share)
        self.last_row = width % ROWS
        self.blocks = 8


def joint_tail(left, right, width):
    lane = lax.broadcasted_iota(jnp.int32, left.shape, 1)
    return jnp.where(lane < width, left, pltpu.roll(right, width, 1))


def deal(tiles, per_chunk, abs_ref):
    for t, tile in enumerate(tiles):
        chunk, at = divmod(t, per_chunk)
        abs_ref[chunk, at * ROWS : (at + 1) * ROWS, :] = tile
    for t in range(len(tiles), per_chunk * abs_ref.shape[0]):
        chunk, at = divmod(t, per_chunk)
        abs_ref[chunk, at * ROWS : (at + 1) * ROWS, :] = jnp.zeros((ROWS, LANES), F32)


def send_graphs(abs_ref, me, keep_ref, give_ref):
    half = keep_ref.shape[0]
    for r, distance in enumerate(distances(half)):
        keep_ref[r] = abs_ref[jnp.bitwise_xor(distance, me)]
        give_ref[r] = abs_ref[jnp.bitwise_xor(distance + 1, me)]


def center_backward(
    plan, grad, att, states, z, unit1, spread1, unit2, spread2,
    out_ref, in_ref, down_ref, bias_ref, gain_ref, layer, me_graph, me_leaf,
    flat_ref, ext_ref, wide1_ref, wide2_ref, abs_ref, keep_ref, give_ref,
):
    cols = columns(bias_ref[:, layer, :])
    gains = columns(gain_ref[layer, :, :])
    share = pl.ds(pl.multiple_of(me_leaf * plan.share_rows, ROWS), plan.share_rows)
    width, hidden = plan.width, plan.hidden

    g_f = normalise_back(grad, gains[:, 1:2], unit2, spread2)
    t = gelu_tanh(z)
    u = gelu(z, t)
    pair_f = split(g_f)
    dz = mul_narrow(split(down_ref[:, layer, :].T), pair_f, NN) * gelu_slope(z, t)
    pair_z = split(dz)
    g_h1 = g_f + mul_narrow(split(plain(in_ref[:, layer, :], flat_ref)), pair_z, NN)
    g_o = normalise_back(g_h1, gains[:, 0:1], unit1, spread1)
    pair_o = split(g_o)
    g_att = mul_narrow(split(plain(out_ref[:, layer, :], flat_ref)), pair_o, NN)

    extend(ext_ref, unit1 * gains[:, 0:1] + cols[:, 2:3])
    wide1_ref[:, 0:hidden] = outer(split(ext_ref[share, :]), pair_z)
    extend(ext_ref, g_f)
    wide2_ref[:, 0:hidden] = outer(split(ext_ref[share, :]), split(u))
    extend(ext_ref, att)
    own_out = outer(split(ext_ref[share, :]), pair_o)

    sums = [lane_sums(v) for v in (g_h1, g_h1 * unit1, g_f, grad, grad * unit2)]
    row = plan.last_tile * ROWS + plan.last_row

    @pl.when(me_leaf == plan.last_owner)
    def _():
        wide2_ref[row + 1 : row + 2, 0:width] = sums[3]
        wide2_ref[row + 2 : row + 3, 0:width] = sums[4]

    tiles = []
    for r in range(plan.share):
        at = slice(r * ROWS, (r + 1) * ROWS)
        for ref in (wide1_ref, wide2_ref):
            tiles += [ref[at, LANES * c : LANES * (c + 1)] for c in range(plan.hid_full)]
        tail = slice(LANES * plan.hid_full, LANES * (plan.hid_full + 1))
        tiles.append(joint_tail(wide1_ref[at, tail], wide2_ref[at, tail], plan.hid_tail))
        for c in range(plan.wid_full + 1):
            tiles.append((r, c))
    wide1_ref[:, 0:width] = own_out

    @pl.when(me_leaf == plan.last_owner)
    def _():
        for n in range(3):
            wide1_ref[row + 1 + n : row + 2 + n, 0:width] = sums[n]

    tiles = [
        wide1_ref[t[0] * ROWS : (t[0] + 1) * ROWS, LANES * t[1] : LANES * (t[1] + 1)]
        if isinstance(t, tuple)
        else t
        for t in tiles
    ]
    deal(tiles, plan.center_tiles, abs_ref)
    send_graphs(abs_ref, me_graph, keep_ref, give_ref)
    return g_att, g_o


def attend_back(att_ref, gatt_ref, q_ref, k_ref, v_ref, s_ref, top, total, slots, ct_ref, p_ref, gq_ref, gk_ref, gv_ref):
    for s in range(slots):
        p_ref[s] = jnp.exp(s_ref[s] - top) / total
    for h in range(HEADS):
        at = slice(HEAD_DIM * h, HEAD_DIM * (h + 1))
        ga, q = gatt_ref[at, :], q_ref[at, :]
        centre = jnp.sum(ga * att_ref[at, :], axis=0, keepdims=True)
        gq = 0.0
        for s in range(slots):
            lanes = slice(LANES * s, LANES * (s + 1))
            k = k_ref[at, lanes]
            p = p_ref[s, h : h + 1, :]
            gp = jnp.sum(ga * v_ref[at, lanes], axis=0, keepdims=True)
            gs = p * (gp - centre) * SCALE
            gv_ref[at, lanes] = p * ga
            gk_ref[at, lanes] = gs * q
            gq += gs * k
        gq_ref[at, :] = gq


def query_gradient(plan, states, gq, me_graph, me_leaf, ext_ref, wide_ref, abs_ref, keep_ref, give_ref):
    share = pl.ds(pl.multiple_of(me_leaf * plan.share_rows, ROWS), plan.share_rows)
    extend(ext_ref, states)
    wide_ref[:, 0 : plan.width] = outer(split(ext_ref[share, :]), split(gq))
    tiles = [
        wide_ref[r * ROWS : (r + 1) * ROWS, LANES * c : LANES * (c + 1)]
        for r in range(plan.share)
        for c in range(plan.query_lanes)
    ]
    deal(tiles, plan.query_tiles, abs_ref)
    send_graphs(abs_ref, me_graph, keep_ref, give_ref)


def live_rows(me_ref, count_ref, slots):
    first = me_ref[1] * slots
    return [count_ref[...] > first + s for s in range(slots)]


def first_kernel(slots, me_ref, count_far, x_far, e_far, h_far, square_far, bias_far,
                 part_ref, q_ref, k_ref, v_ref, s_ref, e1_ref,
                 count_ref, x_ref, e_ref, h_ref, square_ref, bias_ref, w_ref, sems):
    pairs = (
        (x_far, x_ref), (e_far, e_ref), (square_far.at[0:1], square_ref), (bias_far, bias_ref), (h_far, h_ref),
        (count_far, count_ref),
    )
    copies = [pltpu.make_async_copy(far, near, sems.at[n]) for n, (far, near) in enumerate(pairs)]
    for copy in copies:
        copy.start()
    for copy in copies[:2]:
        copy.wait()
    m = slot_cols(x_ref, slots) * slot_cols(e_ref, slots)
    for copy in copies[2:4]:
        copy.wait()
    step = leaf_forward(m, square_ref, bias_ref, 0, k_ref, v_ref)
    for s in range(slots):
        e1_ref[:, s, :] = e_ref[:, s, :] + step[:, LANES * s : LANES * (s + 1)]
    for copy in copies[4:]:
        copy.wait()
    cols = columns(bias_ref[:, 0, :])
    q_ref[...] = mul_narrow(split(square_ref[0, :, 0, :].T), split(h_ref[...]), NN) + cols[:, 0:1]
    attend(q_ref, k_ref, v_ref, live_rows(me_ref, count_ref, slots), s_ref, w_ref, part_ref)


def second_kernel(slots, x_ref, e1_ref, square_ref, bias_ref, k_ref, v_ref, e2_ref):
    m = slot_cols(x_ref, slots) * slot_cols(e1_ref, slots)
    step = leaf_forward(m, square_ref, bias_ref, 1, k_ref, v_ref)
    for s in range(slots):
        e2_ref[:, s, :] = e1_ref[:, s, :] + step[:, LANES * s : LANES * (s + 1)]


def third_kernel(slots, me_ref, count_ref, p0, p1, p2, p3, h_ref, k_ref, v_ref, square_ref, out_ref, in_ref, down_ref,
                 hid_ref, bias_ref, gain_ref,
                 part_ref, att_ref, top_ref, total_ref, unit1_ref, spread1_ref, z_ref, unit2_ref, spread2_ref, h2_ref,
                 q_ref, s_ref, r_ref, w_ref, flat_ref):
    combine([p0, p1, p2, p3], r_ref, att_ref, top_ref, total_ref)
    unit1, spread1, z, unit2, spread2, h2 = center_forward(
        att_ref[...], h_ref[...], out_ref, in_ref, down_ref, hid_ref, bias_ref, gain_ref, 0, flat_ref
    )
    unit1_ref[...] = unit1
    spread1_ref[...] = spread1
    z_ref[...] = z
    unit2_ref[...] = unit2
    spread2_ref[...] = spread2
    h2_ref[...] = h2
    cols = columns(bias_ref[:, 1, :])
    q_ref[...] = mul_narrow(split(square_ref[1, :, 0, :].T), split(h2), NN) + cols[:, 0:1]
    attend(q_ref, k_ref, v_ref, live_rows(me_ref, count_ref, slots), s_ref, w_ref, part_ref)


def fourth_kernel(plan, slots, me_ref, p0, p1, p2, p3, h_ref, q_ref, k_ref, v_ref, s_ref, cot_ref, out_ref, in_ref,
                  down_ref, hid_ref, bias_ref, gain_ref,
                  center_ref, gq_ref, gk_ref, gv_ref, res_ref, keep_ref, give_ref,
                  r_ref, att_ref, top_ref, total_ref, gatt_ref, p_ref, flat_ref, ext_ref, wide1_ref, wide2_ref, abs_ref):
    combine([p0, p1, p2, p3], r_ref, att_ref, top_ref, total_ref)
    unit1, spread1, z, unit2, spread2, out = center_forward(
        att_ref[...], h_ref[...], out_ref, in_ref, down_ref, hid_ref, bias_ref, gain_ref, 1, flat_ref
    )
    center_ref[...] = out
    gatt_ref[...], res_ref[...] = center_backward(
        plan, cot_ref[...], att_ref[...], h_ref[...], z, unit1, spread1, unit2, spread2,
        out_ref, in_ref, down_ref, bias_ref, gain_ref, 1, me_ref[0], me_ref[1],
        flat_ref, ext_ref, wide1_ref, wide2_ref, abs_ref, keep_ref, give_ref,
    )
    attend_back(att_ref, gatt_ref, q_ref, k_ref, v_ref, s_ref, top_ref[...], total_ref[...], slots,
                None, p_ref, gq_ref, gk_ref, gv_ref)


def fifth_kernel(plan, slots, me_ref, x_ref, e_ref, ge_ref, gk_ref, gv_ref,
                 core_ref, give_ref, keep_ref, ext_ref, wide_ref, abs_ref):
    extend(ext_ref, slot_cols(x_ref, slots) * slot_cols(e_ref, slots))
    m = split(ext_ref[...])
    for n, side in enumerate((gk_ref[...], gv_ref[...], slot_cols(ge_ref, slots))):
        wide_ref[n, :, 0 : plan.width] = outer(m, split(side))
    tiles = []
    for r in range(plan.row_tiles):
        at = slice(r * ROWS, (r + 1) * ROWS)
        for n in range(3):
            tiles += [wide_ref[n, at, LANES * c : LANES * (c + 1)] for c in range(plan.wid_full)]
        tail = slice(LANES * plan.wid_full, LANES * (plan.wid_full + 1))
        tiles.append(joint_tail(wide_ref[0, at, tail], wide_ref[1, at, tail], plan.wid_tail))
        tiles.append(wide_ref[2, at, tail])
    deal(tiles, plan.leaf_tiles, abs_ref)
    me_graph, me_leaf = me_ref[0], me_ref[1]
    half = plan.graph_devices // 2
    for other in range(plan.leaf_devices):
        leaf = jnp.bitwise_xor(other, me_leaf)
        for r in range(plan.graph_devices):
            rel = distances(half)[r % half] + r // half
            source = abs_ref[jnp.bitwise_xor(rel, me_graph) * plan.leaf_devices + leaf]
            if other % 2:
                core_ref[other // 2, r] = source
            elif other // 2:
                give_ref[r] = source
            else:
                keep_ref[r] = source


def leaf_back_kernel(slots, layer, last, x_ref, e_ref, ge_ref, *refs):
    if last:
        gx_ref, *refs = refs
    gk_ref, gv_ref, square_ref, new_gx_ref, new_ge_ref, flat_ref = refs
    gm = 0.0
    for n, side in enumerate((gk_ref[...], gv_ref[...], slot_cols(ge_ref, slots))):
        gm += mul_pair(split(plain(square_ref[layer, :, n + 1, :], flat_ref)), split(side), NN)
    for s in range(slots):
        part = gm[:, LANES * s : LANES * (s + 1)]
        gx = part * e_ref[:, s, :]
        new_gx_ref[:, s, :] = gx_ref[:, s, :] + gx if last else gx
        new_ge_ref[:, s, :] = ge_ref[:, s, :] + part * x_ref[:, s, :]


def sixth_kernel(plan, slots, me_ref, g0, g1, g2, g3, res_ref, h2_ref, square_ref,
                 att_ref, h_ref, z_ref, unit1_ref, spread1_ref, unit2_ref, spread2_ref, top_ref, total_ref,
                 q_ref, k_ref, v_ref, s_ref, out_ref, in_ref, down_ref, bias_ref, gain_ref,
                 gq_ref, gk_ref, gv_ref, new_res_ref, keep_ref, give_ref, q_keep_ref, q_give_ref,
                 gatt_ref, p_ref, flat_ref, ext_ref, wide1_ref, wide2_ref, abs_ref, q_abs_ref):
    gq = tree([ref[...] for ref in (g0, g1, g2, g3)], jnp.add)
    grad = res_ref[...] + mul_narrow(split(plain(square_ref[1, :, 0, :], flat_ref)), split(gq), NN)
    query_gradient(plan, h2_ref[...], gq, me_ref[0], me_ref[1], ext_ref, wide1_ref, q_abs_ref, q_keep_ref, q_give_ref)
    gatt_ref[...], new_res_ref[...] = center_backward(
        plan, grad, att_ref[...], h_ref[...], z_ref[...], unit1_ref[...], spread1_ref[...], unit2_ref[...],
        spread2_ref[...], out_ref, in_ref, down_ref, bias_ref, gain_ref, 0, me_ref[0], me_ref[1],
        flat_ref, ext_ref, wide1_ref, wide2_ref, abs_ref, keep_ref, give_ref,
    )
    attend_back(att_ref, gatt_ref, q_ref, k_ref, v_ref, s_ref, top_ref[...], total_ref[...], slots,
                None, p_ref, gq_ref, gk_ref, gv_ref)


def seventh_kernel(plan, me_ref, g0, g1, g2, g3, res_ref, h_ref, square_ref,
                   grad_ref, keep_ref, give_ref, flat_ref, ext_ref, wide_ref, abs_ref):
    gq = tree([ref[...] for ref in (g0, g1, g2, g3)], jnp.add)
    grad_ref[...] = res_ref[...] + mul_narrow(split(plain(square_ref[0, :, 0, :], flat_ref)), split(gq), NN)
    query_gradient(plan, h_ref[...], gq, me_ref[0], me_ref[1], ext_ref, wide_ref, abs_ref, keep_ref, give_ref)


def last_kernel(plan, routes, me_ref, *refs):
    count = len(routes)
    pieces, given, (hid_ref, bias_ref, gain_ref) = refs[:count], refs[count : count + 4], refs[count + 4 : count + 7]
    all_ref, square_ref, out_ref, in_ref, down_ref, sems = refs[count + 7 :]
    me_graph, me_leaf = me_ref[0], me_ref[1]
    width = plan.width
    for ref, (places, first, rows) in zip(pieces, routes):
        for n, (graph, leaf) in enumerate(places):
            all_ref[
                jnp.bitwise_xor(graph, me_graph), jnp.bitwise_xor(leaf, me_leaf), first : first + rows, :
            ] = ref[n]

    def tile(layer, kind, index):
        per = (plan.center_tiles, plan.query_tiles, plan.leaf_tiles)[kind]
        leaf, index = index if kind < 2 else (None, index)
        chunk, at = divmod(index, per)
        if kind == 2:
            chunk, leaf = divmod(chunk, plan.leaf_devices)
        at = (plan.bases[layer][kind] + at) * ROWS
        return all_ref[chunk, leaf, at : at + ROWS, :]

    hid_tail, wid_tail, full, wid = plan.hid_tail, plan.wid_tail, plan.hid_full, plan.wid_full

    def cut(c, whole, tail):
        size = LANES if c < whole else tail
        return slice(LANES * c, LANES * c + size), size

    def row_tile(r, layer):
        leaf, own = divmod(r, plan.share)
        rows = min(ROWS, width - r * ROWS)
        at = slice(r * ROWS, r * ROWS + rows)
        center = [tile(layer, 0, (leaf, own * plan.center_lanes + c)) for c in range(plan.center_lanes)]
        query = [tile(layer, 1, (leaf, own * plan.query_lanes + c)) for c in range(plan.query_lanes)]
        sides = [tile(layer, 2, r * plan.leaf_lanes + c) for c in range(plan.leaf_lanes)]
        tail = center[2 * full]
        ins = center[:full] + [tail]
        downs = center[full : 2 * full] + [pltpu.roll(tail, LANES - hid_tail, 1)]
        outs = center[2 * full + 1 :]
        joint = sides[3 * wid]
        keys = sides[:wid] + [joint]
        values = sides[wid : 2 * wid] + [pltpu.roll(joint, LANES - wid_tail, 1)]
        steps = sides[2 * wid : 3 * wid] + [sides[3 * wid + 1]]
        for c in range(full + 1):
            lanes, size = cut(c, full, hid_tail)
            in_ref[at, layer, lanes] = ins[c][:rows, :size]
            down_ref[at, layer, lanes] = downs[c][:rows, :size]
        for c in range(wid + 1):
            lanes, size = cut(c, wid, wid_tail)
            out_ref[at, layer, lanes] = outs[c][:rows, :size]
            for n, part in enumerate((query, keys, values, steps)):
                square_ref[layer, at, n, lanes] = part[c][:rows, :size]
        if r == width // ROWS:
            first = plan.last_row
            for c in range(full + 1):
                lanes, size = cut(c, full, hid_tail)
                hid_ref[layer : layer + 1, lanes] = ins[c][first : first + 1, :size]
            for c in range(wid + 1):
                lanes, size = cut(c, wid, wid_tail)
                found = ((query, 0), (outs, 0), (outs, 1), (outs, 3), (downs, 1), (values, 0), (steps, 0))
                for n, (part, row) in enumerate(found):
                    bias_ref[n, layer : layer + 1, lanes] = part[c][first + row : first + row + 1, :size]
                gain_ref[layer, 0:1, lanes] = outs[c][first + 2 : first + 3, :size]
                gain_ref[layer, 1:2, lanes] = downs[c][first + 2 : first + 3, :size]

    copies = []
    for block in range(plan.blocks):
        tiles = range(block * plan.row_tiles // plan.blocks, (block + 1) * plan.row_tiles // plan.blocks)
        for r in tiles:
            for layer in range(LAYERS):
                row_tile(r, layer)
        at = pl.ds(tiles.start * ROWS, min(tiles.stop * ROWS, width) - tiles.start * ROWS)
        for n, (here, there) in enumerate(zip((square_ref, out_ref, in_ref, down_ref), given)):
            if n:
                here, there = here.at[at], there.at[at]
            else:
                here, there = here.at[:, at], there.at[:, at]
            copies.append(pltpu.make_async_copy(here, there, sems.at[block, n]))
            copies[-1].start()
    for copy in copies:
        copy.wait()


def after(value, *others):
    return lax.optimization_barrier((value, *others))[0]


def swap(values, axis, size, distance):
    pairs = [(i, i ^ distance) for i in range(size)]
    return jax.tree.map(lambda v: lax.ppermute(v, axis, pairs), values)


def distances(count):
    bits = count.bit_length() - 1
    return [2 * sum(((n >> b) & 1) << (bits - 1 - b) for b in range(bits)) for n in range(count)]


class Clock:
    def __init__(self):
        self.last = ()

    def wait(self, value):
        value = after(value, *self.last)
        self.last = (value,)
        return value

    def mark(self, *values):
        self.last = values


class Stream:
    def __init__(self, chain):
        self.chain, self.result, self.alive = chain, None, True
        self.step()

    def step(self):
        if self.alive:
            try:
                next(self.chain)
            except StopIteration as end:
                self.alive, self.result = False, end.value

    def finish(self):
        while self.alive:
            self.step()
        return self.result


def graph_scatter(clock, keep, give, size):
    own, got = keep, swap(give, "graphs", size, 1)
    distance = 2
    while distance < size:
        yield
        got = clock.wait(got)
        if 2 * distance < size:
            half = own.shape[0] // 2
            far = own[half:] + got[half:]
            own = own[:half] + got[:half]
        else:
            own = own + got
            far = jnp.concatenate([own[1:], own[:1]], axis=0)
        clock.mark(far)
        got = swap(far, "graphs", size, distance)
        distance *= 2
    return own, got


def side_scatter(clock, core, give, keep, queries, sizes):
    got = swap(core, "leaves", sizes[1], 1)
    yield
    got = clock.wait(got)
    far = give + got[1]
    own = keep + got[0]
    clock.mark(far)
    far = swap(far, "leaves", sizes[1], 2)
    yield
    far = clock.wait(far)
    half = own.shape[0] // 2
    q_keep, q_give = queries()
    q_give = jnp.concatenate([q_give, own[half:] + far[half:]], axis=1)
    clock.mark(q_give)
    chain = graph_scatter(
        clock, jnp.concatenate([q_keep, own[:half] + far[:half]], axis=1), q_give, sizes[0]
    )
    return (yield from chain)


def spread(clock, block, places, turns, sizes, first):
    graph_devices, leaf_devices = sizes
    for n, turn in enumerate(turns):
        if turn:
            got, there = swap(block, "graphs", graph_devices, turn), [(g ^ turn, f) for g, f in places]
        else:
            got, there = swap(block, "leaves", leaf_devices, 2), [(g, f ^ 2) for g, f in places]
        if n == len(turns) - 1:
            handed = swap(block, "leaves", leaf_devices, 1)
        yield
        got = clock.wait(got)
        if n < len(turns) - 1:
            block, places = jnp.concatenate([block, got], axis=0), places + there
            clock.mark(block)
    held = ((block, places, 0), (handed, places, 1), (got, there, 0), (swap(got, "leaves", leaf_devices, 1), there, 1))
    return [v for v, _, _ in held], [
        (tuple((g, f ^ flip) for g, f in at), first, block.shape[1]) for _, at, flip in held
    ]


def gather(clock, sums, sizes, first):
    totals = [own + clock.wait(got) for own, got in sums]
    if len(totals) == 1:
        middle = totals[0].shape[1] // 2 // ROWS * ROWS
        totals = [totals[0][:, :middle], totals[0][:, middle:]]
    clock.mark(*totals)
    graph_devices = sizes[0]
    places = [(0, 0), (graph_devices // 2, 0)]
    between = [1 << n for n in range(1, graph_devices.bit_length() - 2)]
    runs = []
    for block, turns in zip(totals, ((1, *between, 0), (0, *between, 1))):
        runs.append(Stream(spread(clock, block, places, turns, sizes, first)))
        first += block.shape[1]
    return runs


def on_device(
    sizes,
    centers,
    leaf_nodes,
    edges,
    leaf_counts,
    square,
    out_proj,
    ff_in,
    ff_out,
    ff_bias,
    biases,
    gains,
    cot_center,
    cot_edges,
):
    graphs, slots, width = leaf_nodes.shape
    hidden = ff_in.shape[2]
    graph_devices, leaf_devices = sizes
    plan = Plan(width, hidden, graph_devices, leaf_devices)
    me = jnp.stack([lax.axis_index("graphs"), lax.axis_index("leaves")]).astype(jnp.int32)

    h = centers.T
    x = leaf_nodes.transpose(2, 1, 0)
    e = edges.transpose(2, 1, 0)
    count = leaf_counts.reshape(1, graphs)
    sq = square.transpose(0, 2, 1, 3)
    wo = out_proj.transpose(1, 0, 2)
    w1 = ff_in.transpose(1, 0, 2)
    w2 = ff_out.transpose(2, 0, 1)
    bias = biases.transpose(1, 0, 2)
    gc = cot_center.T
    ge = cot_edges.transpose(2, 1, 0)

    base = ceil_div(width, ROWS) * ROWS
    wide = plan.share_rows
    lanes = ceil_div(hidden, LANES) * LANES
    shape = lambda *s: jax.ShapeDtypeStruct(s, F32)
    scratch = lambda *s: pltpu.VMEM(s, F32)
    cell = (width, graphs)
    row = (1, graphs)
    flat = (width, lanes)
    sides = (width, slots * graphs)
    cube = (width, slots, graphs)
    heads = (HEAD_ROWS, graphs)
    scores = (slots, HEAD_ROWS, graphs)
    part = (base + 2 * HEAD_ROWS, graphs)
    half = graph_devices // 2

    def call(kernel, ins, outs, scratches, took, first_smem=True):
        return pl.pallas_call(
            kernel,
            in_specs=[SMEM if first_smem and n == 0 else VMEM for n in range(len(ins))],
            out_specs=[VMEM] * len(outs),
            out_shape=[shape(*s) for s in outs],
            scratch_shapes=[scratch(*s) for s in scratches],
            compiler_params=pltpu.CompilerParams(vmem_limit_bytes=KERNEL_VMEM),
            cost_estimate=pl.CostEstimate(flops=int(took * FLOPS_A_US), bytes_accessed=0, transcendentals=0),
        )(*ins)

    def around(value):
        return swap(value, "leaves", leaf_devices, 1), swap(value, "leaves", leaf_devices, 2)

    def all_around(value, near, far):
        return value, near, far, swap(far, "leaves", leaf_devices, 1)

    firsts = (part, cell, sides, sides, scores, cube)
    near_shapes = (cube, cube, cell, (1, width, 4, width), bias.shape)
    part1, q1, k1, v1, s1, e1 = pl.pallas_call(
        functools.partial(first_kernel, slots),
        in_specs=[SMEM] + [HBM] * 6,
        out_specs=[VMEM] * len(firsts),
        out_shape=[shape(*s) for s in firsts],
        scratch_shapes=[
            pltpu.VMEM(count.shape, jnp.int32),
            *[scratch(*s) for s in near_shapes],
            scratch(*scores),
            pltpu.SemaphoreType.DMA((6,)),
        ],
        compiler_params=pltpu.CompilerParams(vmem_limit_bytes=KERNEL_VMEM),
        cost_estimate=pl.CostEstimate(flops=int(5 * FLOPS_A_US), bytes_accessed=0, transcendentals=0),
    )(me, *[pltpu.with_memory_space_constraint(v, pltpu.HBM) for v in (count, x, e, h, sq, bias)])
    near, far = around(part1)
    k2, v2, e2 = call(
        functools.partial(second_kernel, slots), (x, e1, sq, bias), (sides, sides, cube), (), 5, first_smem=False
    )
    parts1 = all_around(part1, near, after(far, k2))
    part2, att1, top1, total1, unit1, spread1, z1, unit2, spread2, h2, q2, s2 = call(
        functools.partial(third_kernel, slots),
        (me, count, *parts1, h, k2, v2, sq, wo, w1, w2, ff_bias, bias, gains),
        (part, cell, heads, heads, cell, row, (hidden, graphs), cell, row, cell, cell, scores),
        ((leaf_devices, *heads), scores, flat),
        8,
    )
    parts2 = all_around(part2, *around(part2))
    center_chunk = (half, plan.center_tiles * ROWS, LANES)
    query_chunk = (half, plan.query_tiles * ROWS, LANES)
    leaf_chunk = (graph_devices, plan.leaf_tiles * ROWS, LANES)
    ext = (wide * leaf_devices, graphs)
    center_out, gq2, gk2, gv2, res2, keep2, give2 = call(
        functools.partial(fourth_kernel, plan, slots),
        (me, *parts2, h2, q2, k2, v2, s2, gc, wo, w1, w2, ff_bias, bias, gains),
        (cell, cell, sides, sides, cell, center_chunk, center_chunk),
        ((leaf_devices, *heads), cell, heads, heads, cell, scores, flat, ext, (wide, lanes), (wide, lanes),
         (graph_devices, *center_chunk[1:])),
        14,
    )
    clock = Clock()
    side_scratch = (
        (plan.row_tiles * ROWS, slots * graphs),
        (3, plan.row_tiles * ROWS, ceil_div(width, LANES) * LANES),
        (graph_devices * leaf_devices, *leaf_chunk[1:]),
    )
    side_shapes = ((2, *leaf_chunk), leaf_chunk, leaf_chunk)

    near, far = around(gq2)
    center2 = Stream(graph_scatter(clock, keep2, give2, graph_devices))
    core2, lgive2, lkeep2 = call(
        functools.partial(fifth_kernel, plan, slots), (me, x, e1, ge, gk2, gv2), side_shapes, side_scratch, 4
    )
    side2 = Stream(side_scatter(clock, core2, lgive2, lkeep2, lambda: (qkeep2, qgive2), sizes))
    gx2, ge1 = call(
        functools.partial(leaf_back_kernel, slots, 1, False),
        (x, e1, ge, after(gk2, core2), gv2, sq),
        (cube, cube),
        (flat,),
        3,
        first_smem=False,
    )
    gqs2 = all_around(gq2, near, after(far, core2))
    gqs2 = (after(gqs2[0], gx2), *gqs2[1:])
    gq1, gk1, gv1, res1, keep1, give1, qkeep2, qgive2 = call(
        functools.partial(sixth_kernel, plan, slots),
        (me, *gqs2, res2, h2, sq, att1, h, z1, unit1, spread1, unit2, spread2, top1, total1,
         q1, k1, v1, s1, wo, w1, w2, bias, gains),
        (cell, sides, sides, cell, center_chunk, center_chunk, query_chunk, query_chunk),
        (cell, scores, flat, ext, (wide, lanes), (wide, lanes),
         (graph_devices, *center_chunk[1:]), (graph_devices, *query_chunk[1:])),
        6,
    )
    near, far = around(gq1)
    center1 = Stream(graph_scatter(clock, keep1, give1, graph_devices))
    clock.mark(gq1)
    center2.step()
    side2.step()
    core1, lgive1, lkeep1 = call(
        functools.partial(fifth_kernel, plan, slots),
        (me, x, e, ge1, after(gk1, *clock.last), gv1),
        side_shapes,
        side_scratch,
        0.4,
    )
    side1 = Stream(side_scatter(clock, core1, lgive1, lkeep1, lambda: (qkeep1, qgive1), sizes))
    clock.mark(core1)
    center2.step()
    center1.step()
    gqs1 = all_around(gq1, near, clock.wait(far))
    side1.step()
    gqs1 = (after(gqs1[0], *clock.last), *gqs1[1:])
    grad_center, qkeep1, qgive1 = call(
        functools.partial(seventh_kernel, plan),
        (me, *gqs1, res1, h, sq),
        (cell, query_chunk, query_chunk),
        (flat, ext, (wide, lanes), (graph_devices, *query_chunk[1:])),
        0.2,
    )
    clock.mark(grad_center)
    side2.step()
    center1.step()
    rows = [0, plan.center_tiles * ROWS, 2 * plan.center_tiles * ROWS]
    c2a, c2b = gather(clock, [center2.finish()], sizes, rows[0])
    side2.step()
    side1.step()
    c2b.step()
    gx1, ge0 = call(
        functools.partial(leaf_back_kernel, slots, 0, True),
        (x, e, ge1, gx2, after(gk1, *clock.last), gv1, sq),
        (cube, cube),
        (flat,),
        0.3,
        first_smem=False,
    )
    clock.mark(gx1)
    c2a.step()
    side1.step()
    c1a, c1b = gather(clock, [center1.finish()], sizes, rows[1])
    for stream in (c2b, side2, side1, c2a, c1b):
        stream.step()
    sa, sb = gather(clock, [side2.finish(), side1.finish()], sizes, rows[2])
    for stream in (c1a, c1b, c2b, sa, sb, c1a, c1b, sb, sa, c2a, c1a, sb, sa):
        stream.step()
    pieces, routes = [], []
    for stream in (c2a, c2b, c1a, c1b, sa, sb):
        found, ways = stream.finish()
        pieces += found
        routes += ways
    large = ((LAYERS, width, 4, width), (width, LAYERS, width), (width, LAYERS, hidden), (width, LAYERS, hidden))
    small = ((LAYERS, hidden), (7, LAYERS, width), (LAYERS, 2, width))
    g_square, g_out, g_in, g_down, g_hid, g_bias, g_gain = pl.pallas_call(
        functools.partial(last_kernel, plan, routes),
        in_specs=[SMEM] + [VMEM] * len(pieces),
        out_specs=[HBM] * len(large) + [VMEM] * len(small),
        out_shape=[shape(*s) for s in large + small],
        scratch_shapes=[
            scratch(graph_devices, leaf_devices, plan.all_tiles * ROWS, LANES),
            *[scratch(*s) for s in large],
            pltpu.SemaphoreType.DMA((plan.blocks, len(large))),
        ],
        compiler_params=pltpu.CompilerParams(vmem_limit_bytes=LAST_VMEM),
    )(me, *pieces)
    return (
        center_out.T,
        e2.transpose(2, 1, 0),
        grad_center.T,
        gx1.transpose(2, 1, 0),
        ge0.transpose(2, 1, 0),
        g_square.transpose(0, 2, 1, 3),
        g_out.transpose(1, 0, 2),
        g_in.transpose(1, 0, 2),
        g_down.transpose(1, 2, 0),
        g_hid,
        g_bias.transpose(1, 0, 2),
        g_gain,
    )


def solution(mesh):
    sizes = (mesh.shape["graphs"], mesh.shape["leaves"])
    in_specs = (
        P("graphs", None),
        P("graphs", "leaves", None),
        P("graphs", "leaves", None),
        P("graphs"),
        P(),
        P(),
        P(),
        P(),
        P(),
        P(),
        P(),
        P("graphs", None),
        P("graphs", "leaves", None),
    )
    out_specs = (
        P("graphs", None),
        P("graphs", "leaves", None),
        P("graphs", None),
        P("graphs", "leaves", None),
        P("graphs", "leaves", None),
        P(),
        P(),
        P(),
        P(),
        P(),
        P(),
        P(),
    )
    return jax.shard_map(
        functools.partial(on_device, sizes),
        mesh=mesh,
        in_specs=in_specs,
        out_specs=out_specs,
        check_vma=False,
    )
```

```python
import functools

import jax
import jax.numpy as jnp
from jax import lax
from jax.experimental import pallas as pl
from jax.experimental.pallas import tpu as pltpu
from jax.sharding import PartitionSpec as P

HEADS = 12
HEAD_DIM = 25
LAYERS = 2
LANES = 128
ROWS = 8
HEAD_ROWS = 16
EPS = 1e-05
KERNEL_VMEM = 24 << 20
LAST_VMEM = 28 << 20
FLOPS_A_US = 5e9
SCALE = HEAD_DIM ** (-0.5)
GELU_A = 0.7978845608028654
GELU_B = 0.044715

F32 = jnp.float32
BF16 = jnp.bfloat16
NN = (((1,), (0,)), ((), ()))
TN = (((0,), (0,)), ((), ()))
NT = (((1,), (1,)), ((), ()))
BOTH = ("graphs", "leaves")
VMEM = pl.BlockSpec(memory_space=pltpu.VMEM)
SMEM = pl.BlockSpec(memory_space=pltpu.SMEM)
HBM = pl.BlockSpec(memory_space=pltpu.HBM)


def ceil_div(a, b):
    return -(-a // b)


def dot(a, b, dims):
    return lax.dot_general(a, b, dims, preferred_element_type=F32)


def split(v):
    high = v.astype(BF16)
    return high, (v - high.astype(F32)).astype(BF16)


def mul_pair(a, b, dims):
    return dot(a[0], b[0], dims) + (dot(a[0], b[1], dims) + dot(a[1], b[0], dims))


def mul_narrow(a, b, dims):
    width = b[0].shape[1]
    both = dot(a[0], jnp.concatenate(b, axis=1), dims)
    return both[:, :width] + (both[:, width:] + dot(a[1], b[0], dims))


def outer(a, b):
    left = jnp.concatenate([a[0], a[0], a[1]], axis=1)
    right = jnp.concatenate([b[0], b[1], b[0]], axis=1)
    return dot(left, right, NT)


def lane_sums(v):
    ones = jnp.ones((ROWS, v.shape[1]), BF16)
    high, low = split(v)
    return (dot(ones, high, NT) + dot(ones, low, NT))[0:1, :]


def columns(rows):
    count = rows.shape[0]
    if count % ROWS:
        fill = jnp.zeros((ROWS - count % ROWS, rows.shape[1]), F32)
        rows = jnp.concatenate([rows, fill], axis=0)
    return rows.T


def plain(value, ref):
    rows, lanes = value.shape
    ref[0:rows, 0:lanes] = value
    return ref[0:rows, 0:lanes]


def slot_cols(ref, slots):
    return jnp.concatenate([ref[:, s, :] for s in range(slots)], axis=1)


def leaf_forward(m, square_ref, bias_ref, layer, k_ref, v_ref):
    pair = split(m)
    cols = columns(bias_ref[:, layer, :])
    k_ref[...] = mul_pair(split(square_ref[layer, :, 1, :].T), pair, NN)
    v_ref[...] = mul_pair(split(square_ref[layer, :, 2, :].T), pair, NN) + cols[:, 5:6]
    return mul_pair(split(square_ref[layer, :, 3, :].T), pair, NN) + cols[:, 6:7]


def attend(q_ref, k_ref, v_ref, live, s_ref, w_ref, part_ref):
    slots = len(live)
    s_ref[...] = jnp.zeros(s_ref.shape, F32)
    for h in range(HEADS):
        at = slice(HEAD_DIM * h, HEAD_DIM * (h + 1))
        q = q_ref[at, :]
        for s in range(slots):
            k = k_ref[at, LANES * s : LANES * (s + 1)]
            s_ref[s, h : h + 1, :] = jnp.sum(q * k, axis=0, keepdims=True)
    scores = [jnp.where(live[s], s_ref[s] * SCALE, -1e30) for s in range(slots)]
    top = functools.reduce(jnp.maximum, scores)
    weights = [jnp.where(live[s], jnp.exp(scores[s] - top), 0.0) for s in range(slots)]
    for s in range(slots):
        s_ref[s] = scores[s]
        w_ref[s] = weights[s]
    for h in range(HEADS):
        at = slice(HEAD_DIM * h, HEAD_DIM * (h + 1))
        total = 0.0
        for s in range(slots):
            total += w_ref[s, h : h + 1, :] * v_ref[at, LANES * s : LANES * (s + 1)]
        part_ref[at, :] = total
    width = HEADS * HEAD_DIM
    base = ceil_div(width, ROWS) * ROWS
    part_ref[width:base, :] = jnp.zeros((base - width, LANES), F32)
    part_ref[base : base + HEAD_ROWS, :] = functools.reduce(jnp.add, weights)
    part_ref[base + HEAD_ROWS : base + 2 * HEAD_ROWS, :] = top


def tree(values, op):
    while len(values) > 1:
        values = [op(values[i], values[i + 1]) for i in range(0, len(values), 2)]
    return values[0]


def combine(part_refs, r_ref, att_ref, top_ref, total_ref):
    base = ceil_div(HEADS * HEAD_DIM, ROWS) * ROWS
    totals = [ref[base : base + HEAD_ROWS, :] for ref in part_refs]
    tops = [ref[base + HEAD_ROWS : base + 2 * HEAD_ROWS, :] for ref in part_refs]
    top = tree(tops, jnp.maximum)
    factors = [jnp.exp(t - top) for t in tops]
    total = tree([a * b for a, b in zip(totals, factors)], jnp.add)
    head = lax.broadcasted_iota(jnp.int32, total.shape, 0) < HEADS
    total = jnp.where(head, total, 1.0)
    top_ref[...] = top
    total_ref[...] = total
    for n, factor in enumerate(factors):
        r_ref[n] = factor / total
    for h in range(HEADS):
        at = slice(HEAD_DIM * h, HEAD_DIM * (h + 1))
        att_ref[at, :] = tree(
            [ref[at, :] * r_ref[n, h : h + 1, :] for n, ref in enumerate(part_refs)], jnp.add
        )


def normalise(v):
    centred = v - jnp.mean(v, axis=0, keepdims=True)
    spread = lax.rsqrt(jnp.mean(centred * centred, axis=0, keepdims=True) + EPS)
    return centred * spread, spread


def normalise_back(grad, gain, unit, spread):
    g = grad * gain
    return spread * (
        g - jnp.mean(g, axis=0, keepdims=True) - unit * jnp.mean(g * unit, axis=0, keepdims=True)
    )


def gelu_tanh(z):
    return jnp.tanh(GELU_A * (z + GELU_B * (z * z * z)))


def gelu(z, t):
    return 0.5 * z * (1.0 + t)


def gelu_slope(z, t):
    return 0.5 * (1.0 + t) + 0.5 * z * (1.0 - t * t) * (GELU_A * (1.0 + 3.0 * GELU_B * (z * z)))


def center_forward(att, states, out_ref, in_ref, down_ref, hid_ref, bias_ref, gain_ref, layer, flat_ref):
    cols = columns(bias_ref[:, layer, :])
    gains = columns(gain_ref[layer, :, :])
    hid = columns(hid_ref[layer : layer + 1, :])
    o = mul_narrow(split(out_ref[:, layer, :].T), split(att), NN) + cols[:, 1:2]
    unit1, spread1 = normalise(states + o)
    h1 = unit1 * gains[:, 0:1] + cols[:, 2:3]
    z = mul_narrow(split(in_ref[:, layer, :].T), split(h1), NN) + hid[:, 0:1]
    u = gelu(z, gelu_tanh(z))
    f = mul_narrow(split(plain(down_ref[:, layer, :], flat_ref)), split(u), NN) + cols[:, 3:4]
    unit2, spread2 = normalise(h1 + f)
    return unit1, spread1, z, unit2, spread2, unit2 * gains[:, 1:2] + cols[:, 4:5]


def extend(ref, value):
    rows, width = ref.shape[0], value.shape[0]
    ref[width:rows, :] = jnp.where(
        lax.broadcasted_iota(jnp.int32, (rows - width, value.shape[1]), 0) == 0, 1.0, 0.0
    )
    ref[0:width, :] = value


TURNS = {"c2": "zxy", "cs": "xzy", "s1": "yxz"}
ORDER = (
    "C2", "leaf_weights", "S2", "C2", "query_far", "C1", "S1", "S2", "query_weights", "c2", "C1", "S1", "S2", "c2a",
    "c2b", "S2", "S1", "c2a", "cs", "S1", "c2b", "csa", "csb", "c2a", "s1", "s1b", "s1a", "csa", "c2b", "csb", "s1b",
    "leaf_messages", "s1a", "s1b", "csa", "s1a", "csb",
)


class Plan:
    def __init__(self, width, hidden, graph_devices, leaf_devices):
        self.width, self.hidden = width, hidden
        self.graph_devices, self.leaf_devices = graph_devices, leaf_devices
        self.row_tiles = ceil_div(width + 4, ROWS)
        self.share = ceil_div(self.row_tiles, leaf_devices)
        self.share_rows = self.share * ROWS
        self.hid_full, self.hid_tail = divmod(hidden, LANES)
        self.wid_full, self.wid_tail = divmod(width, LANES)
        self.center_lanes = 2 * self.hid_full + 1 + self.wid_full + 1
        self.center_tiles = ceil_div(self.share * self.center_lanes, graph_devices)
        self.query_lanes = self.wid_full + 1
        self.query_tiles = ceil_div(self.share * self.query_lanes, graph_devices)
        self.leaf_lanes = 3 * self.wid_full + 2
        self.leaf_tiles = ceil_div(self.row_tiles * self.leaf_lanes, graph_devices * leaf_devices)
        self.side_tiles = self.query_tiles + self.leaf_tiles
        self.all_tiles = 2 * (self.center_tiles + self.side_tiles)
        side = (2 * self.center_tiles + self.side_tiles, 2 * self.center_tiles)
        self.bases = [
            (self.center_tiles if layer == 0 else 0, side[layer], side[layer] + self.query_tiles) for layer in (0, 1)
        ]
        self.last_owner, self.last_tile = divmod(width // ROWS, self.share)
        self.last_row = width % ROWS
        self.blocks = 8


def joint_tail(left, right, width):
    lane = lax.broadcasted_iota(jnp.int32, left.shape, 1)
    return jnp.where(lane < width, left, pltpu.roll(right, width, 1))


def deal(tiles, per_chunk, abs_ref):
    for t, tile in enumerate(tiles):
        chunk, at = divmod(t, per_chunk)
        abs_ref[chunk, at * ROWS : (at + 1) * ROWS, :] = tile
    for t in range(len(tiles), per_chunk * abs_ref.shape[0]):
        chunk, at = divmod(t, per_chunk)
        abs_ref[chunk, at * ROWS : (at + 1) * ROWS, :] = jnp.zeros((ROWS, LANES), F32)


def send_graphs(abs_ref, me, keep_ref, give_ref):
    half = keep_ref.shape[0]
    for r, distance in enumerate(distances(half)):
        keep_ref[r] = abs_ref[jnp.bitwise_xor(distance, me)]
        give_ref[r] = abs_ref[jnp.bitwise_xor(distance + 1, me)]


def center_backward(
    plan, grad, att, states, z, unit1, spread1, unit2, spread2,
    out_ref, in_ref, down_ref, bias_ref, gain_ref, layer, me_graph, me_leaf,
    flat_ref, ext_ref, wide1_ref, wide2_ref, abs_ref, keep_ref, give_ref,
):
    cols = columns(bias_ref[:, layer, :])
    gains = columns(gain_ref[layer, :, :])
    share = pl.ds(pl.multiple_of(me_leaf * plan.share_rows, ROWS), plan.share_rows)
    width, hidden = plan.width, plan.hidden

    g_f = normalise_back(grad, gains[:, 1:2], unit2, spread2)
    t = gelu_tanh(z)
    u = gelu(z, t)
    pair_f = split(g_f)
    dz = mul_narrow(split(down_ref[:, layer, :].T), pair_f, NN) * gelu_slope(z, t)
    pair_z = split(dz)
    g_h1 = g_f + mul_narrow(split(plain(in_ref[:, layer, :], flat_ref)), pair_z, NN)
    g_o = normalise_back(g_h1, gains[:, 0:1], unit1, spread1)
    pair_o = split(g_o)
    g_att = mul_narrow(split(plain(out_ref[:, layer, :], flat_ref)), pair_o, NN)

    extend(ext_ref, unit1 * gains[:, 0:1] + cols[:, 2:3])
    wide1_ref[:, 0:hidden] = outer(split(ext_ref[share, :]), pair_z)
    extend(ext_ref, g_f)
    wide2_ref[:, 0:hidden] = outer(split(ext_ref[share, :]), split(u))
    extend(ext_ref, att)
    own_out = outer(split(ext_ref[share, :]), pair_o)

    sums = [lane_sums(v) for v in (g_h1, g_h1 * unit1, g_f, grad, grad * unit2)]
    row = plan.last_tile * ROWS + plan.last_row

    @pl.when(me_leaf == plan.last_owner)
    def _():
        wide2_ref[row + 1 : row + 2, 0:width] = sums[3]
        wide2_ref[row + 2 : row + 3, 0:width] = sums[4]

    tiles = []
    for r in range(plan.share):
        at = slice(r * ROWS, (r + 1) * ROWS)
        for ref in (wide1_ref, wide2_ref):
            tiles += [ref[at, LANES * c : LANES * (c + 1)] for c in range(plan.hid_full)]
        tail = slice(LANES * plan.hid_full, LANES * (plan.hid_full + 1))
        tiles.append(joint_tail(wide1_ref[at, tail], wide2_ref[at, tail], plan.hid_tail))
        for c in range(plan.wid_full + 1):
            tiles.append((r, c))
    wide1_ref[:, 0:width] = own_out

    @pl.when(me_leaf == plan.last_owner)
    def _():
        for n in range(3):
            wide1_ref[row + 1 + n : row + 2 + n, 0:width] = sums[n]

    tiles = [
        wide1_ref[t[0] * ROWS : (t[0] + 1) * ROWS, LANES * t[1] : LANES * (t[1] + 1)]
        if isinstance(t, tuple)
        else t
        for t in tiles
    ]
    deal(tiles, plan.center_tiles, abs_ref)
    send_graphs(abs_ref, me_graph, keep_ref, give_ref)
    return g_att, g_o


def attend_back(att_ref, gatt_ref, q_ref, k_ref, v_ref, s_ref, top, total, slots, ct_ref, p_ref, gq_ref, gk_ref, gv_ref):
    for s in range(slots):
        p_ref[s] = jnp.exp(s_ref[s] - top) / total
    for h in range(HEADS):
        at = slice(HEAD_DIM * h, HEAD_DIM * (h + 1))
        ga, q = gatt_ref[at, :], q_ref[at, :]
        centre = jnp.sum(ga * att_ref[at, :], axis=0, keepdims=True)
        gq = 0.0
        for s in range(slots):
            lanes = slice(LANES * s, LANES * (s + 1))
            k = k_ref[at, lanes]
            p = p_ref[s, h : h + 1, :]
            gp = jnp.sum(ga * v_ref[at, lanes], axis=0, keepdims=True)
            gs = p * (gp - centre) * SCALE
            gv_ref[at, lanes] = p * ga
            gk_ref[at, lanes] = gs * q
            gq += gs * k
        gq_ref[at, :] = gq


def query_gradient(plan, states, gq, me_graph, me_leaf, ext_ref, wide_ref, abs_ref, keep_ref, give_ref):
    share = pl.ds(pl.multiple_of(me_leaf * plan.share_rows, ROWS), plan.share_rows)
    extend(ext_ref, states)
    wide_ref[:, 0 : plan.width] = outer(split(ext_ref[share, :]), split(gq))
    tiles = [
        wide_ref[r * ROWS : (r + 1) * ROWS, LANES * c : LANES * (c + 1)]
        for r in range(plan.share)
        for c in range(plan.query_lanes)
    ]
    deal(tiles, plan.query_tiles, abs_ref)
    send_graphs(abs_ref, me_graph, keep_ref, give_ref)


def live_rows(me_ref, count_ref, slots):
    first = me_ref[1] * slots
    return [count_ref[...] > first + s for s in range(slots)]


def first_kernel(slots, me_ref, count_far, x_far, e_far, h_far, square_far, bias_far,
                 part_ref, q_ref, k_ref, v_ref, s_ref, e1_ref,
                 count_ref, x_ref, e_ref, h_ref, square_ref, bias_ref, w_ref, sems):
    pairs = (
        (x_far, x_ref), (e_far, e_ref), (square_far.at[0:1], square_ref), (bias_far, bias_ref), (h_far, h_ref),
        (count_far, count_ref),
    )
    copies = [pltpu.make_async_copy(far, near, sems.at[n]) for n, (far, near) in enumerate(pairs)]
    for copy in copies:
        copy.start()
    for copy in copies[:2]:
        copy.wait()
    m = slot_cols(x_ref, slots) * slot_cols(e_ref, slots)
    for copy in copies[2:4]:
        copy.wait()
    step = leaf_forward(m, square_ref, bias_ref, 0, k_ref, v_ref)
    for s in range(slots):
        e1_ref[:, s, :] = e_ref[:, s, :] + step[:, LANES * s : LANES * (s + 1)]
    for copy in copies[4:]:
        copy.wait()
    cols = columns(bias_ref[:, 0, :])
    q_ref[...] = mul_narrow(split(square_ref[0, :, 0, :].T), split(h_ref[...]), NN) + cols[:, 0:1]
    attend(q_ref, k_ref, v_ref, live_rows(me_ref, count_ref, slots), s_ref, w_ref, part_ref)


def second_kernel(slots, x_ref, e1_ref, square_ref, bias_ref, k_ref, v_ref, e2_ref):
    m = slot_cols(x_ref, slots) * slot_cols(e1_ref, slots)
    step = leaf_forward(m, square_ref, bias_ref, 1, k_ref, v_ref)
    for s in range(slots):
        e2_ref[:, s, :] = e1_ref[:, s, :] + step[:, LANES * s : LANES * (s + 1)]


def third_kernel(slots, me_ref, count_ref, p0, p1, p2, p3, h_ref, k_ref, v_ref, square_ref, out_ref, in_ref, down_ref,
                 hid_ref, bias_ref, gain_ref,
                 part_ref, att_ref, top_ref, total_ref, unit1_ref, spread1_ref, z_ref, unit2_ref, spread2_ref, h2_ref,
                 q_ref, s_ref, r_ref, w_ref, flat_ref):
    combine([p0, p1, p2, p3], r_ref, att_ref, top_ref, total_ref)
    unit1, spread1, z, unit2, spread2, h2 = center_forward(
        att_ref[...], h_ref[...], out_ref, in_ref, down_ref, hid_ref, bias_ref, gain_ref, 0, flat_ref
    )
    unit1_ref[...] = unit1
    spread1_ref[...] = spread1
    z_ref[...] = z
    unit2_ref[...] = unit2
    spread2_ref[...] = spread2
    h2_ref[...] = h2
    cols = columns(bias_ref[:, 1, :])
    q_ref[...] = mul_narrow(split(square_ref[1, :, 0, :].T), split(h2), NN) + cols[:, 0:1]
    attend(q_ref, k_ref, v_ref, live_rows(me_ref, count_ref, slots), s_ref, w_ref, part_ref)


def fourth_kernel(plan, slots, me_ref, p0, p1, p2, p3, h_ref, q_ref, k_ref, v_ref, s_ref, cot_ref, out_ref, in_ref,
                  down_ref, hid_ref, bias_ref, gain_ref,
                  center_ref, gq_ref, gk_ref, gv_ref, res_ref, keep_ref, give_ref,
                  r_ref, att_ref, top_ref, total_ref, gatt_ref, p_ref, flat_ref, ext_ref, wide1_ref, wide2_ref, abs_ref):
    combine([p0, p1, p2, p3], r_ref, att_ref, top_ref, total_ref)
    unit1, spread1, z, unit2, spread2, out = center_forward(
        att_ref[...], h_ref[...], out_ref, in_ref, down_ref, hid_ref, bias_ref, gain_ref, 1, flat_ref
    )
    center_ref[...] = out
    gatt_ref[...], res_ref[...] = center_backward(
        plan, cot_ref[...], att_ref[...], h_ref[...], z, unit1, spread1, unit2, spread2,
        out_ref, in_ref, down_ref, bias_ref, gain_ref, 1, me_ref[0], me_ref[1],
        flat_ref, ext_ref, wide1_ref, wide2_ref, abs_ref, keep_ref, give_ref,
    )
    attend_back(att_ref, gatt_ref, q_ref, k_ref, v_ref, s_ref, top_ref[...], total_ref[...], slots,
                None, p_ref, gq_ref, gk_ref, gv_ref)


def fifth_kernel(plan, slots, me_ref, x_ref, e_ref, ge_ref, gk_ref, gv_ref,
                 core_ref, give_ref, keep_ref, ext_ref, wide_ref, abs_ref):
    extend(ext_ref, slot_cols(x_ref, slots) * slot_cols(e_ref, slots))
    m = split(ext_ref[...])
    for n, side in enumerate((gk_ref[...], gv_ref[...], slot_cols(ge_ref, slots))):
        wide_ref[n, :, 0 : plan.width] = outer(m, split(side))
    tiles = []
    for r in range(plan.row_tiles):
        at = slice(r * ROWS, (r + 1) * ROWS)
        for n in range(3):
            tiles += [wide_ref[n, at, LANES * c : LANES * (c + 1)] for c in range(plan.wid_full)]
        tail = slice(LANES * plan.wid_full, LANES * (plan.wid_full + 1))
        tiles.append(joint_tail(wide_ref[0, at, tail], wide_ref[1, at, tail], plan.wid_tail))
        tiles.append(wide_ref[2, at, tail])
    deal(tiles, plan.leaf_tiles, abs_ref)
    me_graph, me_leaf = me_ref[0], me_ref[1]
    half = plan.graph_devices // 2
    for other in range(plan.leaf_devices):
        leaf = jnp.bitwise_xor(other, me_leaf)
        for r in range(plan.graph_devices):
            rel = distances(half)[r % half] + r // half
            source = abs_ref[jnp.bitwise_xor(rel, me_graph) * plan.leaf_devices + leaf]
            if other % 2:
                core_ref[other // 2, r] = source
            elif other // 2:
                give_ref[r] = source
            else:
                keep_ref[r] = source


def leaf_back_kernel(slots, layer, last, x_ref, e_ref, ge_ref, *refs):
    if last:
        gx_ref, *refs = refs
    gk_ref, gv_ref, square_ref, new_gx_ref, new_ge_ref, flat_ref = refs
    gm = 0.0
    for n, side in enumerate((gk_ref[...], gv_ref[...], slot_cols(ge_ref, slots))):
        gm += mul_pair(split(plain(square_ref[layer, :, n + 1, :], flat_ref)), split(side), NN)
    for s in range(slots):
        part = gm[:, LANES * s : LANES * (s + 1)]
        gx = part * e_ref[:, s, :]
        new_gx_ref[:, s, :] = gx_ref[:, s, :] + gx if last else gx
        new_ge_ref[:, s, :] = ge_ref[:, s, :] + part * x_ref[:, s, :]


def sixth_kernel(plan, slots, me_ref, g0, g1, g2, g3, res_ref, h2_ref, square_ref,
                 att_ref, h_ref, z_ref, unit1_ref, spread1_ref, unit2_ref, spread2_ref, top_ref, total_ref,
                 q_ref, k_ref, v_ref, s_ref, out_ref, in_ref, down_ref, bias_ref, gain_ref,
                 gq_ref, gk_ref, gv_ref, new_res_ref, keep_ref, give_ref, q_keep_ref, q_give_ref,
                 gatt_ref, p_ref, flat_ref, ext_ref, wide1_ref, wide2_ref, abs_ref, q_abs_ref):
    gq = tree([ref[...] for ref in (g0, g1, g2, g3)], jnp.add)
    grad = res_ref[...] + mul_narrow(split(plain(square_ref[1, :, 0, :], flat_ref)), split(gq), NN)
    query_gradient(plan, h2_ref[...], gq, me_ref[0], me_ref[1], ext_ref, wide1_ref, q_abs_ref, q_keep_ref, q_give_ref)
    gatt_ref[...], new_res_ref[...] = center_backward(
        plan, grad, att_ref[...], h_ref[...], z_ref[...], unit1_ref[...], spread1_ref[...], unit2_ref[...],
        spread2_ref[...], out_ref, in_ref, down_ref, bias_ref, gain_ref, 0, me_ref[0], me_ref[1],
        flat_ref, ext_ref, wide1_ref, wide2_ref, abs_ref, keep_ref, give_ref,
    )
    attend_back(att_ref, gatt_ref, q_ref, k_ref, v_ref, s_ref, top_ref[...], total_ref[...], slots,
                None, p_ref, gq_ref, gk_ref, gv_ref)


def seventh_kernel(plan, me_ref, g0, g1, g2, g3, res_ref, h_ref, square_ref,
                   grad_ref, keep_ref, give_ref, flat_ref, ext_ref, wide_ref, abs_ref):
    gq = tree([ref[...] for ref in (g0, g1, g2, g3)], jnp.add)
    grad_ref[...] = res_ref[...] + mul_narrow(split(plain(square_ref[0, :, 0, :], flat_ref)), split(gq), NN)
    query_gradient(plan, h_ref[...], gq, me_ref[0], me_ref[1], ext_ref, wide_ref, abs_ref, keep_ref, give_ref)


def last_kernel(plan, routes, me_ref, *refs):
    count = len(routes)
    pieces, given, (hid_ref, bias_ref, gain_ref) = refs[:count], refs[count : count + 4], refs[count + 4 : count + 7]
    all_ref, square_ref, out_ref, in_ref, down_ref, sems = refs[count + 7 :]
    me_graph, me_leaf = me_ref[0], me_ref[1]
    width = plan.width
    for ref, (places, first, rows) in zip(pieces, routes):
        for n, (graph, leaf) in enumerate(places):
            all_ref[
                jnp.bitwise_xor(graph, me_graph), jnp.bitwise_xor(leaf, me_leaf), first : first + rows, :
            ] = ref[n]

    def tile(layer, kind, index):
        per = (plan.center_tiles, plan.query_tiles, plan.leaf_tiles)[kind]
        leaf, index = index if kind < 2 else (None, index)
        chunk, at = divmod(index, per)
        if kind == 2:
            chunk, leaf = divmod(chunk, plan.leaf_devices)
        at = (plan.bases[layer][kind] + at) * ROWS
        return all_ref[chunk, leaf, at : at + ROWS, :]

    hid_tail, wid_tail, full, wid = plan.hid_tail, plan.wid_tail, plan.hid_full, plan.wid_full

    def cut(c, whole, tail):
        size = LANES if c < whole else tail
        return slice(LANES * c, LANES * c + size), size

    def row_tile(r, layer):
        leaf, own = divmod(r, plan.share)
        rows = min(ROWS, width - r * ROWS)
        at = slice(r * ROWS, r * ROWS + rows)
        center = [tile(layer, 0, (leaf, own * plan.center_lanes + c)) for c in range(plan.center_lanes)]
        query = [tile(layer, 1, (leaf, own * plan.query_lanes + c)) for c in range(plan.query_lanes)]
        sides = [tile(layer, 2, r * plan.leaf_lanes + c) for c in range(plan.leaf_lanes)]
        tail = center[2 * full]
        ins = center[:full] + [tail]
        downs = center[full : 2 * full] + [pltpu.roll(tail, LANES - hid_tail, 1)]
        outs = center[2 * full + 1 :]
        joint = sides[3 * wid]
        keys = sides[:wid] + [joint]
        values = sides[wid : 2 * wid] + [pltpu.roll(joint, LANES - wid_tail, 1)]
        steps = sides[2 * wid : 3 * wid] + [sides[3 * wid + 1]]
        for c in range(full + 1):
            lanes, size = cut(c, full, hid_tail)
            in_ref[at, layer, lanes] = ins[c][:rows, :size]
            down_ref[at, layer, lanes] = downs[c][:rows, :size]
        for c in range(wid + 1):
            lanes, size = cut(c, wid, wid_tail)
            out_ref[at, layer, lanes] = outs[c][:rows, :size]
            for n, part in enumerate((query, keys, values, steps)):
                square_ref[layer, at, n, lanes] = part[c][:rows, :size]
        if r == width // ROWS:
            first = plan.last_row
            for c in range(full + 1):
                lanes, size = cut(c, full, hid_tail)
                hid_ref[layer : layer + 1, lanes] = ins[c][first : first + 1, :size]
            for c in range(wid + 1):
                lanes, size = cut(c, wid, wid_tail)
                found = ((query, 0), (outs, 0), (outs, 1), (outs, 3), (downs, 1), (values, 0), (steps, 0))
                for n, (part, row) in enumerate(found):
                    bias_ref[n, layer : layer + 1, lanes] = part[c][first + row : first + row + 1, :size]
                gain_ref[layer, 0:1, lanes] = outs[c][first + 2 : first + 3, :size]
                gain_ref[layer, 1:2, lanes] = downs[c][first + 2 : first + 3, :size]

    copies = []
    for block in range(plan.blocks):
        tiles = range(block * plan.row_tiles // plan.blocks, (block + 1) * plan.row_tiles // plan.blocks)
        for r in tiles:
            for layer in range(LAYERS):
                row_tile(r, layer)
        at = pl.ds(tiles.start * ROWS, min(tiles.stop * ROWS, width) - tiles.start * ROWS)
        for n, (here, there) in enumerate(zip((square_ref, out_ref, in_ref, down_ref), given)):
            if n:
                here, there = here.at[at], there.at[at]
            else:
                here, there = here.at[:, at], there.at[:, at]
            copies.append(pltpu.make_async_copy(here, there, sems.at[block, n]))
            copies[-1].start()
    for copy in copies:
        copy.wait()


def after(value, *others):
    return lax.optimization_barrier((value, *others))[0]


def swap(values, axis, size, distance):
    pairs = [(i, i ^ distance) for i in range(size)]
    return jax.tree.map(lambda v: lax.ppermute(v, axis, pairs), values)


def distances(count):
    bits = count.bit_length() - 1
    return [2 * sum(((n >> b) & 1) << (bits - 1 - b) for b in range(bits)) for n in range(count)]


class Clock:
    def __init__(self):
        self.last = ()

    def wait(self, value):
        value = after(value, *self.last)
        self.last = (value,)
        return value

    def mark(self, *values):
        self.last = values


class Stream:
    def __init__(self, chain):
        self.chain, self.result, self.alive = chain, None, True
        self.step()

    def step(self):
        if self.alive:
            try:
                next(self.chain)
            except StopIteration as end:
                self.alive, self.result = False, end.value

    def finish(self):
        while self.alive:
            self.step()
        return self.result


def graph_scatter(clock, keep, give, size):
    own, got = keep, swap(give, "graphs", size, 1)
    distance = 2
    while distance < size:
        yield
        got = clock.wait(got)
        if 2 * distance < size:
            half = own.shape[0] // 2
            far = own[half:] + got[half:]
            own = own[:half] + got[:half]
        else:
            own = own + got
            far = jnp.concatenate([own[1:], own[:1]], axis=0)
        clock.mark(far)
        got = swap(far, "graphs", size, distance)
        distance *= 2
    return own, got


def side_scatter(clock, core, give, keep, queries, sizes):
    got = swap(core, "leaves", sizes[1], 1)
    yield
    got = clock.wait(got)
    far = give + got[1]
    own = keep + got[0]
    clock.mark(far)
    far = swap(far, "leaves", sizes[1], 2)
    yield
    far = clock.wait(far)
    half = own.shape[0] // 2
    q_keep, q_give = queries()
    q_give = jnp.concatenate([q_give, own[half:] + far[half:]], axis=1)
    clock.mark(q_give)
    chain = graph_scatter(
        clock, jnp.concatenate([q_keep, own[:half] + far[:half]], axis=1), q_give, sizes[0]
    )
    return (yield from chain)


class Spread:
    def __init__(self, clock, block, turns, sizes, first, early):
        self.clock, self.sizes, self.first, self.early = clock, sizes, first, early
        self.block, self.turns = block, turns
        self.places = [(0, 0), (sizes[0] // 2, 0)]
        self.near = self.far = None
        self.send()

    def send(self):
        turn = self.turns[0]
        if turn:
            self.got = swap(self.block, "graphs", self.sizes[0], turn)
            self.there = [(g ^ turn, f) for g, f in self.places]
        else:
            self.got = swap(self.block, "leaves", self.sizes[1], 2)
            self.there = [(g, f ^ 2) for g, f in self.places]
        if self.early and len(self.turns) == 1:
            self.give_near = swap(self.block, "leaves", self.sizes[1], 1)

    def step(self):
        if not self.turns:
            return
        got = self.clock.wait(self.got)
        self.turns = self.turns[1:]
        if self.turns:
            self.block = jnp.concatenate([self.block, got], axis=0)
            self.places = self.places + self.there
            self.clock.mark(self.block)
            self.send()
        else:
            self.got = got
            self.give_far = swap(got, "leaves", self.sizes[1], 1)

    def give(self):
        while len(self.turns) > 1:
            self.step()
        self.give_near = swap(after(self.block, *self.clock.last), "leaves", self.sizes[1], 1)

    def take_near(self):
        self.near = self.clock.wait(self.give_near)

    def take_far(self):
        while self.turns:
            self.step()
        self.far = self.clock.wait(self.give_far)

    def pieces(self):
        while self.turns:
            self.step()
        if self.near is None:
            self.near = self.give_near
        if self.far is None:
            self.far = self.give_far
        flipped = [[(g, f ^ 1) for g, f in at] for at in (self.places, self.there)]
        values = (self.block, self.near, self.got, self.far)
        return [
            (v, tuple(at), self.first)
            for v, at in zip(values, (self.places, flipped[0], self.there, flipped[1]))
        ]


def gather(clock, sums, turns, sizes, first, early, late):
    totals = [own + clock.wait(got) for own, got in sums]
    if len(totals) == 1 or totals[0].shape != totals[1].shape:
        total = jnp.concatenate(totals, axis=1)
        middle = total.shape[1] // 2 // ROWS * ROWS
        totals = [total[:, :middle], total[:, middle:]]
    clock.mark(*totals)
    ways = {"x": [0], "y": [1], "z": [1 << n for n in range(1, sizes[0].bit_length() - 2)]}
    chains = []
    for block, order in zip(totals, (turns, turns.translate(str.maketrans("xy", "yx")))):
        chains.append((block, [way for turn in order for way in ways[turn]], sizes, first, early))
        first += block.shape[1]
    (block, *rest), later = chains
    run = Spread(clock, block, *rest)
    if late:
        return run, lambda: Spread(clock, after(later[0], *clock.last), *later[1:])
    return run, Spread(clock, *later)


def on_device(
    sizes,
    centers,
    leaf_nodes,
    edges,
    leaf_counts,
    square,
    out_proj,
    ff_in,
    ff_out,
    ff_bias,
    biases,
    gains,
    cot_center,
    cot_edges,
):
    graphs, slots, width = leaf_nodes.shape
    hidden = ff_in.shape[2]
    graph_devices, leaf_devices = sizes
    plan = Plan(width, hidden, graph_devices, leaf_devices)
    me = jnp.stack([lax.axis_index("graphs"), lax.axis_index("leaves")]).astype(jnp.int32)

    h = centers.T
    x = leaf_nodes.transpose(2, 1, 0)
    e = edges.transpose(2, 1, 0)
    count = leaf_counts.reshape(1, graphs)
    sq = square.transpose(0, 2, 1, 3)
    wo = out_proj.transpose(1, 0, 2)
    w1 = ff_in.transpose(1, 0, 2)
    w2 = ff_out.transpose(2, 0, 1)
    bias = biases.transpose(1, 0, 2)
    gc = cot_center.T
    ge = cot_edges.transpose(2, 1, 0)

    base = ceil_div(width, ROWS) * ROWS
    wide = plan.share_rows
    lanes = ceil_div(hidden, LANES) * LANES
    shape = lambda *s: jax.ShapeDtypeStruct(s, F32)
    scratch = lambda *s: pltpu.VMEM(s, F32)
    cell = (width, graphs)
    row = (1, graphs)
    flat = (width, lanes)
    sides = (width, slots * graphs)
    cube = (width, slots, graphs)
    heads = (HEAD_ROWS, graphs)
    scores = (slots, HEAD_ROWS, graphs)
    part = (base + 2 * HEAD_ROWS, graphs)
    half = graph_devices // 2

    def call(kernel, ins, outs, scratches, took, first_smem=True):
        return pl.pallas_call(
            kernel,
            in_specs=[SMEM if first_smem and n == 0 else VMEM for n in range(len(ins))],
            out_specs=[VMEM] * len(outs),
            out_shape=[shape(*s) for s in outs],
            scratch_shapes=[scratch(*s) for s in scratches],
            compiler_params=pltpu.CompilerParams(vmem_limit_bytes=KERNEL_VMEM),
            cost_estimate=pl.CostEstimate(flops=int(took * FLOPS_A_US), bytes_accessed=0, transcendentals=0),
        )(*ins)

    def around(value):
        return swap(value, "leaves", leaf_devices, 1), swap(value, "leaves", leaf_devices, 2)

    def all_around(value, near, far):
        return value, near, far, swap(far, "leaves", leaf_devices, 1)

    firsts = (part, cell, sides, sides, scores, cube)
    near_shapes = (cube, cube, cell, (1, width, 4, width), bias.shape)
    part1, q1, k1, v1, s1, e1 = pl.pallas_call(
        functools.partial(first_kernel, slots),
        in_specs=[SMEM] + [HBM] * 6,
        out_specs=[VMEM] * len(firsts),
        out_shape=[shape(*s) for s in firsts],
        scratch_shapes=[
            pltpu.VMEM(count.shape, jnp.int32),
            *[scratch(*s) for s in near_shapes],
            scratch(*scores),
            pltpu.SemaphoreType.DMA((6,)),
        ],
        compiler_params=pltpu.CompilerParams(vmem_limit_bytes=KERNEL_VMEM),
        cost_estimate=pl.CostEstimate(flops=int(5 * FLOPS_A_US), bytes_accessed=0, transcendentals=0),
    )(me, *[pltpu.with_memory_space_constraint(v, pltpu.HBM) for v in (count, x, e, h, sq, bias)])
    near, far = around(part1)
    k2, v2, e2 = call(
        functools.partial(second_kernel, slots), (x, e1, sq, bias), (sides, sides, cube), (), 5, first_smem=False
    )
    parts1 = all_around(part1, near, after(far, k2))
    part2, att1, top1, total1, unit1, spread1, z1, unit2, spread2, h2, q2, s2 = call(
        functools.partial(third_kernel, slots),
        (me, count, *parts1, h, k2, v2, sq, wo, w1, w2, ff_bias, bias, gains),
        (part, cell, heads, heads, cell, row, (hidden, graphs), cell, row, cell, cell, scores),
        ((leaf_devices, *heads), scores, flat),
        8,
    )
    parts2 = all_around(part2, *around(part2))
    center_chunk = (half, plan.center_tiles * ROWS, LANES)
    query_chunk = (half, plan.query_tiles * ROWS, LANES)
    leaf_chunk = (graph_devices, plan.leaf_tiles * ROWS, LANES)
    ext = (wide * leaf_devices, graphs)
    center_out, gq2, gk2, gv2, res2, keep2, give2 = call(
        functools.partial(fourth_kernel, plan, slots),
        (me, *parts2, h2, q2, k2, v2, s2, gc, wo, w1, w2, ff_bias, bias, gains),
        (cell, cell, sides, sides, cell, center_chunk, center_chunk),
        ((leaf_devices, *heads), cell, heads, heads, cell, scores, flat, ext, (wide, lanes), (wide, lanes),
         (graph_devices, *center_chunk[1:])),
        14,
    )
    clock = Clock()
    side_scratch = (
        (plan.row_tiles * ROWS, slots * graphs),
        (3, plan.row_tiles * ROWS, ceil_div(width, LANES) * LANES),
        (graph_devices * leaf_devices, *leaf_chunk[1:]),
    )
    side_shapes = ((2, *leaf_chunk), leaf_chunk, leaf_chunk)

    near, far = around(gq2)
    center2 = Stream(graph_scatter(clock, keep2, give2, graph_devices))
    core2, lgive2, lkeep2 = call(
        functools.partial(fifth_kernel, plan, slots), (me, x, e1, ge, gk2, gv2), side_shapes, side_scratch, 4
    )
    side2 = Stream(side_scatter(clock, core2, lgive2, lkeep2, lambda: (qkeep2, qgive2), sizes))
    gx2, ge1 = call(
        functools.partial(leaf_back_kernel, slots, 1, False),
        (x, e1, ge, after(gk2, core2), gv2, sq),
        (cube, cube),
        (flat,),
        3,
        first_smem=False,
    )
    gqs2 = all_around(gq2, near, after(far, core2))
    gqs2 = (after(gqs2[0], gx2), *gqs2[1:])
    gq1, gk1, gv1, res1, keep1, give1, qkeep2, qgive2 = call(
        functools.partial(sixth_kernel, plan, slots),
        (me, *gqs2, res2, h2, sq, att1, h, z1, unit1, spread1, unit2, spread2, top1, total1,
         q1, k1, v1, s1, wo, w1, w2, bias, gains),
        (cell, sides, sides, cell, center_chunk, center_chunk, query_chunk, query_chunk),
        (cell, scores, flat, ext, (wide, lanes), (wide, lanes),
         (graph_devices, *center_chunk[1:]), (graph_devices, *query_chunk[1:])),
        6,
    )
    near, far = around(gq1)
    center1 = Stream(graph_scatter(clock, keep1, give1, graph_devices))
    clock.mark(gq1)
    done = {}

    def leaf_weights():
        sent = call(
            functools.partial(fifth_kernel, plan, slots),
            (me, x, e, ge1, after(gk1, *clock.last), gv1),
            side_shapes,
            side_scratch,
            0.4,
        )
        clock.mark(sent[0])
        streams["S1"] = Stream(side_scatter(clock, *sent, lambda: done["queries"], sizes))

    def leaf_messages():
        done["leaf"] = call(
            functools.partial(leaf_back_kernel, slots, 0, True),
            (x, e, ge1, gx2, after(gk1, *clock.last), gv1, sq),
            (cube, cube),
            (flat,),
            0.3,
            first_smem=False,
        )
        clock.mark(done["leaf"][0])

    def query_near():
        done["near"] = clock.wait(near)

    def query_far():
        done["far"] = clock.wait(far)
        done["hop"] = swap(done["far"], "leaves", leaf_devices, 1)

    def query_weights():
        hop = clock.wait(done["hop"])
        arrived = done.get("near", near)
        done["center"], *done["queries"] = call(
            functools.partial(seventh_kernel, plan),
            (me, gq1, arrived, done["far"], hop, res1, h, sq),
            (cell, query_chunk, query_chunk),
            (flat, ext, (wide, lanes), (graph_devices, *query_chunk[1:])),
            0.2,
        )
        clock.mark(done["center"])

    streams = {"C2": center2, "C1": center1, "S2": side2}
    kernels = {
        "leaf_weights": leaf_weights,
        "leaf_messages": leaf_messages,
        "query_near": query_near,
        "query_far": query_far,
        "query_weights": query_weights,
    }
    groups = {"c2": ("C2",), "c1": ("C1",), "cs": ("C1", "S2"), "s": ("S2", "S1"), "s2": ("S2",), "s1": ("S1",)}
    firsts = {"C2": 0, "C1": plan.center_tiles, "S2": 2 * plan.center_tiles}
    firsts["S1"] = firsts["S2"] + plan.side_tiles
    for step in ORDER:
        name, mark = step.rstrip("<>!"), step[len(step.rstrip("<>!")) :]
        if name in kernels:
            kernels[name]()
        elif name in groups:
            parts = groups[name]
            streams[name + "a"], streams[name + "b"] = gather(
                clock,
                [streams[part].finish() for part in parts],
                TURNS[name],
                sizes,
                firsts[parts[0]] * ROWS,
                name + "a>" not in ORDER,
                name + "b!" in ORDER,
            )
        elif mark == "!":
            streams[name] = streams[name]()
        else:
            getattr(streams[name], {"": "step", ">": "give", "<": "take_near", "<<": "take_far"}[mark])()
    (gx1, ge0), grad_center = done["leaf"], done["center"]
    pieces, routes = [], []
    for name in (group + half for group in TURNS for half in "ab"):
        for piece, places, first in streams[name].pieces():
            pieces.append(piece)
            routes.append((places, first, piece.shape[1]))
    large = ((LAYERS, width, 4, width), (width, LAYERS, width), (width, LAYERS, hidden), (width, LAYERS, hidden))
    small = ((LAYERS, hidden), (7, LAYERS, width), (LAYERS, 2, width))
    g_square, g_out, g_in, g_down, g_hid, g_bias, g_gain = pl.pallas_call(
        functools.partial(last_kernel, plan, routes),
        in_specs=[SMEM] + [VMEM] * len(pieces),
        out_specs=[HBM] * len(large) + [VMEM] * len(small),
        out_shape=[shape(*s) for s in large + small],
        scratch_shapes=[
            scratch(graph_devices, leaf_devices, plan.all_tiles * ROWS, LANES),
            *[scratch(*s) for s in large],
            pltpu.SemaphoreType.DMA((plan.blocks, len(large))),
        ],
        compiler_params=pltpu.CompilerParams(vmem_limit_bytes=LAST_VMEM),
    )(me, *pieces)
    return (
        center_out.T,
        e2.transpose(2, 1, 0),
        grad_center.T,
        gx1.transpose(2, 1, 0),
        ge0.transpose(2, 1, 0),
        g_square.transpose(0, 2, 1, 3),
        g_out.transpose(1, 0, 2),
        g_in.transpose(1, 0, 2),
        g_down.transpose(1, 2, 0),
        g_hid,
        g_bias.transpose(1, 0, 2),
        g_gain,
    )


def solution(mesh):
    sizes = (mesh.shape["graphs"], mesh.shape["leaves"])
    in_specs = (
        P("graphs", None),
        P("graphs", "leaves", None),
        P("graphs", "leaves", None),
        P("graphs"),
        P(),
        P(),
        P(),
        P(),
        P(),
        P(),
        P(),
        P("graphs", None),
        P("graphs", "leaves", None),
    )
    out_specs = (
        P("graphs", None),
        P("graphs", "leaves", None),
        P("graphs", None),
        P("graphs", "leaves", None),
        P("graphs", "leaves", None),
        P(),
        P(),
        P(),
        P(),
        P(),
        P(),
        P(),
    )
    return jax.shard_map(
        functools.partial(on_device, sizes),
        mesh=mesh,
        in_specs=in_specs,
        out_specs=out_specs,
        check_vma=False,
    )
```

```python
import functools

import jax
import jax.numpy as jnp
from jax import lax
from jax.experimental import pallas as pl
from jax.experimental.pallas import tpu as pltpu
from jax.sharding import PartitionSpec as P

HEADS = 12
HEAD_DIM = 25
LAYERS = 2
LANES = 128
ROWS = 8
HEAD_ROWS = 16
EPS = 1e-05
KERNEL_VMEM = 24 << 20
LAST_VMEM = 28 << 20
FLOPS_A_US = 5e9
SCALE = HEAD_DIM ** (-0.5)
GELU_A = 0.7978845608028654
GELU_B = 0.044715

F32 = jnp.float32
BF16 = jnp.bfloat16
NN = (((1,), (0,)), ((), ()))
TN = (((0,), (0,)), ((), ()))
NT = (((1,), (1,)), ((), ()))
BOTH = ("graphs", "leaves")
VMEM = pl.BlockSpec(memory_space=pltpu.VMEM)
SMEM = pl.BlockSpec(memory_space=pltpu.SMEM)
HBM = pl.BlockSpec(memory_space=pltpu.HBM)


def ceil_div(a, b):
    return -(-a // b)


def dot(a, b, dims):
    return lax.dot_general(a, b, dims, preferred_element_type=F32)


def split(v):
    high = v.astype(BF16)
    return high, (v - high.astype(F32)).astype(BF16)


def mul_pair(a, b, dims):
    return dot(a[0], b[0], dims) + (dot(a[0], b[1], dims) + dot(a[1], b[0], dims))


def mul_narrow(a, b, dims):
    width = b[0].shape[1]
    both = dot(a[0], jnp.concatenate(b, axis=1), dims)
    return both[:, :width] + (both[:, width:] + dot(a[1], b[0], dims))


def outer(a, b):
    left = jnp.concatenate([a[0], a[0], a[1]], axis=1)
    right = jnp.concatenate([b[0], b[1], b[0]], axis=1)
    return dot(left, right, NT)


def lane_sums(v):
    ones = jnp.ones((ROWS, v.shape[1]), BF16)
    high, low = split(v)
    return (dot(ones, high, NT) + dot(ones, low, NT))[0:1, :]


def columns(rows):
    count = rows.shape[0]
    if count % ROWS:
        fill = jnp.zeros((ROWS - count % ROWS, rows.shape[1]), F32)
        rows = jnp.concatenate([rows, fill], axis=0)
    return rows.T


def plain(value, ref):
    rows, lanes = value.shape
    ref[0:rows, 0:lanes] = value
    return ref[0:rows, 0:lanes]


def slot_cols(ref, slots):
    return jnp.concatenate([ref[:, s, :] for s in range(slots)], axis=1)


def leaf_forward(m, square_ref, bias_ref, layer, k_ref, v_ref):
    pair = split(m)
    cols = columns(bias_ref[:, layer, :])
    k_ref[...] = mul_pair(split(square_ref[layer, :, 1, :].T), pair, NN)
    v_ref[...] = mul_pair(split(square_ref[layer, :, 2, :].T), pair, NN) + cols[:, 5:6]
    return mul_pair(split(square_ref[layer, :, 3, :].T), pair, NN) + cols[:, 6:7]


def attend(q_ref, k_ref, v_ref, live, s_ref, w_ref, part_ref):
    slots = len(live)
    s_ref[...] = jnp.zeros(s_ref.shape, F32)
    for h in range(HEADS):
        at = slice(HEAD_DIM * h, HEAD_DIM * (h + 1))
        q = q_ref[at, :]
        for s in range(slots):
            k = k_ref[at, LANES * s : LANES * (s + 1)]
            s_ref[s, h : h + 1, :] = jnp.sum(q * k, axis=0, keepdims=True)
    scores = [jnp.where(live[s], s_ref[s] * SCALE, -1e30) for s in range(slots)]
    top = functools.reduce(jnp.maximum, scores)
    weights = [jnp.where(live[s], jnp.exp(scores[s] - top), 0.0) for s in range(slots)]
    for s in range(slots):
        s_ref[s] = scores[s]
        w_ref[s] = weights[s]
    for h in range(HEADS):
        at = slice(HEAD_DIM * h, HEAD_DIM * (h + 1))
        total = 0.0
        for s in range(slots):
            total += w_ref[s, h : h + 1, :] * v_ref[at, LANES * s : LANES * (s + 1)]
        part_ref[at, :] = total
    width = HEADS * HEAD_DIM
    base = ceil_div(width, ROWS) * ROWS
    part_ref[width:base, :] = jnp.zeros((base - width, LANES), F32)
    part_ref[base : base + HEAD_ROWS, :] = functools.reduce(jnp.add, weights)
    part_ref[base + HEAD_ROWS : base + 2 * HEAD_ROWS, :] = top


def tree(values, op):
    while len(values) > 1:
        values = [op(values[i], values[i + 1]) for i in range(0, len(values), 2)]
    return values[0]


def combine(part_refs, r_ref, att_ref, top_ref, total_ref):
    base = ceil_div(HEADS * HEAD_DIM, ROWS) * ROWS
    totals = [ref[base : base + HEAD_ROWS, :] for ref in part_refs]
    tops = [ref[base + HEAD_ROWS : base + 2 * HEAD_ROWS, :] for ref in part_refs]
    top = tree(tops, jnp.maximum)
    factors = [jnp.exp(t - top) for t in tops]
    total = tree([a * b for a, b in zip(totals, factors)], jnp.add)
    head = lax.broadcasted_iota(jnp.int32, total.shape, 0) < HEADS
    total = jnp.where(head, total, 1.0)
    top_ref[...] = top
    total_ref[...] = total
    for n, factor in enumerate(factors):
        r_ref[n] = factor / total
    for h in range(HEADS):
        at = slice(HEAD_DIM * h, HEAD_DIM * (h + 1))
        att_ref[at, :] = tree(
            [ref[at, :] * r_ref[n, h : h + 1, :] for n, ref in enumerate(part_refs)], jnp.add
        )


def normalise(v):
    centred = v - jnp.mean(v, axis=0, keepdims=True)
    spread = lax.rsqrt(jnp.mean(centred * centred, axis=0, keepdims=True) + EPS)
    return centred * spread, spread


def normalise_back(grad, gain, unit, spread):
    g = grad * gain
    return spread * (
        g - jnp.mean(g, axis=0, keepdims=True) - unit * jnp.mean(g * unit, axis=0, keepdims=True)
    )


def gelu_tanh(z):
    return jnp.tanh(GELU_A * (z + GELU_B * (z * z * z)))


def gelu(z, t):
    return 0.5 * z * (1.0 + t)


def gelu_slope(z, t):
    return 0.5 * (1.0 + t) + 0.5 * z * (1.0 - t * t) * (GELU_A * (1.0 + 3.0 * GELU_B * (z * z)))


def center_forward(att, states, out_ref, in_ref, down_ref, hid_ref, bias_ref, gain_ref, layer, flat_ref):
    cols = columns(bias_ref[:, layer, :])
    gains = columns(gain_ref[layer, :, :])
    hid = columns(hid_ref[layer : layer + 1, :])
    o = mul_narrow(split(out_ref[:, layer, :].T), split(att), NN) + cols[:, 1:2]
    unit1, spread1 = normalise(states + o)
    h1 = unit1 * gains[:, 0:1] + cols[:, 2:3]
    z = mul_narrow(split(in_ref[:, layer, :].T), split(h1), NN) + hid[:, 0:1]
    u = gelu(z, gelu_tanh(z))
    f = mul_narrow(split(plain(down_ref[:, layer, :], flat_ref)), split(u), NN) + cols[:, 3:4]
    unit2, spread2 = normalise(h1 + f)
    return unit1, spread1, z, unit2, spread2, unit2 * gains[:, 1:2] + cols[:, 4:5]


def extend(ref, value):
    rows, width = ref.shape[0], value.shape[0]
    ref[width:rows, :] = jnp.where(
        lax.broadcasted_iota(jnp.int32, (rows - width, value.shape[1]), 0) == 0, 1.0, 0.0
    )
    ref[0:width, :] = value


TURNS = {"c2": "zxy", "cs": "xzy", "s1": "xyz"}
ORDER = (
    "C2", "S2", "upper_messages", "leaf_weights", "C2", "query_far", "C1", "S1", "S2", "query_weights",
    "leaf_messages", "c2", "C1", "S1", "S2", "c2a", "c2b", "S2", "S1", "c2a", "cs", "S1", "c2b", "csa", "csb", "c2a",
    "s1", "c2b", "s1b", "s1a", "csa", "csb", "s1b", "s1a", "s1b", "csa", "s1a", "csb",
)


class Plan:
    def __init__(self, width, hidden, graph_devices, leaf_devices):
        self.width, self.hidden = width, hidden
        self.graph_devices, self.leaf_devices = graph_devices, leaf_devices
        self.row_tiles = ceil_div(width + 4, ROWS)
        self.share = ceil_div(self.row_tiles, leaf_devices)
        self.share_rows = self.share * ROWS
        self.hid_full, self.hid_tail = divmod(hidden, LANES)
        self.wid_full, self.wid_tail = divmod(width, LANES)
        self.center_lanes = 2 * self.hid_full + 1 + self.wid_full + 1
        self.center_tiles = ceil_div(self.share * self.center_lanes, graph_devices)
        self.query_lanes = self.wid_full + 1
        self.query_tiles = ceil_div(self.share * self.query_lanes, graph_devices)
        self.leaf_lanes = 3 * self.wid_full + 2
        self.leaf_tiles = ceil_div(self.row_tiles * self.leaf_lanes, graph_devices * leaf_devices)
        self.side_tiles = self.query_tiles + self.leaf_tiles
        self.all_tiles = 2 * (self.center_tiles + self.side_tiles)
        side = (2 * self.center_tiles + self.side_tiles, 2 * self.center_tiles)
        self.bases = [
            (self.center_tiles if layer == 0 else 0, side[layer], side[layer] + self.query_tiles) for layer in (0, 1)
        ]
        self.last_owner, self.last_tile = divmod(width // ROWS, self.share)
        self.last_row = width % ROWS
        self.blocks = 8


def joint_tail(left, right, width):
    lane = lax.broadcasted_iota(jnp.int32, left.shape, 1)
    return jnp.where(lane < width, left, pltpu.roll(right, width, 1))


def deal(tiles, per_chunk, abs_ref):
    for t, tile in enumerate(tiles):
        chunk, at = divmod(t, per_chunk)
        abs_ref[chunk, at * ROWS : (at + 1) * ROWS, :] = tile
    for t in range(len(tiles), per_chunk * abs_ref.shape[0]):
        chunk, at = divmod(t, per_chunk)
        abs_ref[chunk, at * ROWS : (at + 1) * ROWS, :] = jnp.zeros((ROWS, LANES), F32)


def send_graphs(abs_ref, me, keep_ref, give_ref):
    half = keep_ref.shape[0]
    for r, distance in enumerate(distances(half)):
        keep_ref[r] = abs_ref[jnp.bitwise_xor(distance, me)]
        give_ref[r] = abs_ref[jnp.bitwise_xor(distance + 1, me)]


def center_backward(
    grad, z, unit1, spread1, unit2, spread2, out_ref, in_ref, down_ref, bias_ref, gain_ref, layer, flat_ref
):
    gains = columns(gain_ref[layer, :, :])
    g_f = normalise_back(grad, gains[:, 1:2], unit2, spread2)
    dz = mul_narrow(split(down_ref[:, layer, :].T), split(g_f), NN) * gelu_slope(z, gelu_tanh(z))
    g_h1 = g_f + mul_narrow(split(plain(in_ref[:, layer, :], flat_ref)), split(dz), NN)
    g_o = normalise_back(g_h1, gains[:, 0:1], unit1, spread1)
    g_att = mul_narrow(split(plain(out_ref[:, layer, :], flat_ref)), split(g_o), NN)
    return g_att, g_o, g_f, dz, g_h1


def center_weights(
    plan, grad, att, z, unit1, unit2, g_o, g_f, dz, g_h1, bias_ref, gain_ref, layer, me_graph, me_leaf,
    ext_ref, wide1_ref, wide2_ref, abs_ref, keep_ref, give_ref,
):
    cols = columns(bias_ref[:, layer, :])
    gains = columns(gain_ref[layer, :, :])
    share = pl.ds(pl.multiple_of(me_leaf * plan.share_rows, ROWS), plan.share_rows)
    width, hidden = plan.width, plan.hidden
    u = gelu(z, gelu_tanh(z))

    extend(ext_ref, unit1 * gains[:, 0:1] + cols[:, 2:3])
    wide1_ref[:, 0:hidden] = outer(split(ext_ref[share, :]), split(dz))
    extend(ext_ref, g_f)
    wide2_ref[:, 0:hidden] = outer(split(ext_ref[share, :]), split(u))
    extend(ext_ref, att)
    own_out = outer(split(ext_ref[share, :]), split(g_o))

    sums = [lane_sums(v) for v in (g_h1, g_h1 * unit1, g_f, grad, grad * unit2)]
    row = plan.last_tile * ROWS + plan.last_row

    @pl.when(me_leaf == plan.last_owner)
    def _():
        wide2_ref[row + 1 : row + 2, 0:width] = sums[3]
        wide2_ref[row + 2 : row + 3, 0:width] = sums[4]

    tiles = []
    for r in range(plan.share):
        at = slice(r * ROWS, (r + 1) * ROWS)
        for ref in (wide1_ref, wide2_ref):
            tiles += [ref[at, LANES * c : LANES * (c + 1)] for c in range(plan.hid_full)]
        tail = slice(LANES * plan.hid_full, LANES * (plan.hid_full + 1))
        tiles.append(joint_tail(wide1_ref[at, tail], wide2_ref[at, tail], plan.hid_tail))
        for c in range(plan.wid_full + 1):
            tiles.append((r, c))
    wide1_ref[:, 0:width] = own_out

    @pl.when(me_leaf == plan.last_owner)
    def _():
        for n in range(3):
            wide1_ref[row + 1 + n : row + 2 + n, 0:width] = sums[n]

    tiles = [
        wide1_ref[t[0] * ROWS : (t[0] + 1) * ROWS, LANES * t[1] : LANES * (t[1] + 1)]
        if isinstance(t, tuple)
        else t
        for t in tiles
    ]
    deal(tiles, plan.center_tiles, abs_ref)
    send_graphs(abs_ref, me_graph, keep_ref, give_ref)


def attend_back(att_ref, gatt_ref, q_ref, k_ref, v_ref, s_ref, top, total, slots, ct_ref, p_ref, gq_ref, gk_ref, gv_ref):
    for s in range(slots):
        p_ref[s] = jnp.exp(s_ref[s] - top) / total
    for h in range(HEADS):
        at = slice(HEAD_DIM * h, HEAD_DIM * (h + 1))
        ga, q = gatt_ref[at, :], q_ref[at, :]
        centre = jnp.sum(ga * att_ref[at, :], axis=0, keepdims=True)
        gq = 0.0
        for s in range(slots):
            lanes = slice(LANES * s, LANES * (s + 1))
            k = k_ref[at, lanes]
            p = p_ref[s, h : h + 1, :]
            gp = jnp.sum(ga * v_ref[at, lanes], axis=0, keepdims=True)
            gs = p * (gp - centre) * SCALE
            gv_ref[at, lanes] = p * ga
            gk_ref[at, lanes] = gs * q
            gq += gs * k
        gq_ref[at, :] = gq


def query_gradient(plan, states, gq, me_graph, me_leaf, ext_ref, wide_ref, abs_ref, keep_ref, give_ref):
    share = pl.ds(pl.multiple_of(me_leaf * plan.share_rows, ROWS), plan.share_rows)
    extend(ext_ref, states)
    wide_ref[:, 0 : plan.width] = outer(split(ext_ref[share, :]), split(gq))
    tiles = [
        wide_ref[r * ROWS : (r + 1) * ROWS, LANES * c : LANES * (c + 1)]
        for r in range(plan.share)
        for c in range(plan.query_lanes)
    ]
    deal(tiles, plan.query_tiles, abs_ref)
    send_graphs(abs_ref, me_graph, keep_ref, give_ref)


def live_rows(me_ref, count_ref, slots):
    first = me_ref[1] * slots
    return [count_ref[...] > first + s for s in range(slots)]


def first_kernel(slots, me_ref, count_far, x_far, e_far, h_far, square_far, bias_far,
                 part_ref, q_ref, k_ref, v_ref, s_ref, e1_ref,
                 count_ref, x_ref, e_ref, h_ref, square_ref, bias_ref, w_ref, sems):
    pairs = (
        (x_far, x_ref), (e_far, e_ref), (square_far.at[0:1], square_ref), (bias_far, bias_ref), (h_far, h_ref),
        (count_far, count_ref),
    )
    copies = [pltpu.make_async_copy(far, near, sems.at[n]) for n, (far, near) in enumerate(pairs)]
    for copy in copies:
        copy.start()
    for copy in copies[:2]:
        copy.wait()
    m = slot_cols(x_ref, slots) * slot_cols(e_ref, slots)
    for copy in copies[2:4]:
        copy.wait()
    step = leaf_forward(m, square_ref, bias_ref, 0, k_ref, v_ref)
    for s in range(slots):
        e1_ref[:, s, :] = e_ref[:, s, :] + step[:, LANES * s : LANES * (s + 1)]
    for copy in copies[4:]:
        copy.wait()
    cols = columns(bias_ref[:, 0, :])
    q_ref[...] = mul_narrow(split(square_ref[0, :, 0, :].T), split(h_ref[...]), NN) + cols[:, 0:1]
    attend(q_ref, k_ref, v_ref, live_rows(me_ref, count_ref, slots), s_ref, w_ref, part_ref)


def second_kernel(slots, x_ref, e1_ref, square_ref, bias_ref, k_ref, v_ref, e2_ref):
    m = slot_cols(x_ref, slots) * slot_cols(e1_ref, slots)
    step = leaf_forward(m, square_ref, bias_ref, 1, k_ref, v_ref)
    for s in range(slots):
        e2_ref[:, s, :] = e1_ref[:, s, :] + step[:, LANES * s : LANES * (s + 1)]


def third_kernel(slots, me_ref, count_ref, p0, p1, p2, p3, h_ref, k_ref, v_ref, square_ref, out_ref, in_ref, down_ref,
                 hid_ref, bias_ref, gain_ref,
                 part_ref, att_ref, top_ref, total_ref, unit1_ref, spread1_ref, z_ref, unit2_ref, spread2_ref, h2_ref,
                 q_ref, s_ref, r_ref, w_ref, flat_ref):
    combine([p0, p1, p2, p3], r_ref, att_ref, top_ref, total_ref)
    unit1, spread1, z, unit2, spread2, h2 = center_forward(
        att_ref[...], h_ref[...], out_ref, in_ref, down_ref, hid_ref, bias_ref, gain_ref, 0, flat_ref
    )
    unit1_ref[...] = unit1
    spread1_ref[...] = spread1
    z_ref[...] = z
    unit2_ref[...] = unit2
    spread2_ref[...] = spread2
    h2_ref[...] = h2
    cols = columns(bias_ref[:, 1, :])
    q_ref[...] = mul_narrow(split(square_ref[1, :, 0, :].T), split(h2), NN) + cols[:, 0:1]
    attend(q_ref, k_ref, v_ref, live_rows(me_ref, count_ref, slots), s_ref, w_ref, part_ref)


def edge_kernel(slots, layer, x_ref, e_ref, ge_ref, square_ref, step_ref, weight_ref, flat_ref, ext_ref):
    extend(ext_ref, slot_cols(x_ref, slots) * slot_cols(e_ref, slots))
    side = split(slot_cols(ge_ref, slots))
    step_ref[...] = mul_pair(split(plain(square_ref[layer, :, 3, :], flat_ref)), side, NN)
    weight_ref[:, 0 : square_ref.shape[3]] = outer(split(ext_ref[...]), side)


def fourth_kernel(slots, p0, p1, p2, p3, h_ref, q_ref, k_ref, v_ref, s_ref, cot_ref, out_ref, in_ref,
                  down_ref, hid_ref, bias_ref, gain_ref,
                  center_ref, gq_ref, gk_ref, gv_ref, res_ref, att_ref, z_ref, unit1_ref, unit2_ref, gf_ref, dz_ref, gh1_ref,
                  r_ref, top_ref, total_ref, gatt_ref, p_ref, flat_ref):
    combine([p0, p1, p2, p3], r_ref, att_ref, top_ref, total_ref)
    unit1_ref[...], spread1, z_ref[...], unit2_ref[...], spread2, center_ref[...] = center_forward(
        att_ref[...], h_ref[...], out_ref, in_ref, down_ref, hid_ref, bias_ref, gain_ref, 1, flat_ref
    )
    gatt_ref[...], res_ref[...], gf_ref[...], dz_ref[...], gh1_ref[...] = center_backward(
        cot_ref[...], z_ref[...], unit1_ref[...], spread1, unit2_ref[...], spread2,
        out_ref, in_ref, down_ref, bias_ref, gain_ref, 1, flat_ref,
    )
    attend_back(att_ref, gatt_ref, q_ref, k_ref, v_ref, s_ref, top_ref[...], total_ref[...], slots,
                None, p_ref, gq_ref, gk_ref, gv_ref)


def weights_kernel(plan, me_ref, cot_ref, att_ref, z_ref, unit1_ref, unit2_ref, res_ref, gf_ref, dz_ref, gh1_ref,
                   bias_ref, gain_ref, keep_ref, give_ref, ext_ref, wide1_ref, wide2_ref, abs_ref):
    center_weights(
        plan, cot_ref[...], att_ref[...], z_ref[...], unit1_ref[...], unit2_ref[...], res_ref[...], gf_ref[...],
        dz_ref[...], gh1_ref[...], bias_ref, gain_ref, 1, me_ref[0], me_ref[1],
        ext_ref, wide1_ref, wide2_ref, abs_ref, keep_ref, give_ref,
    )


def fifth_kernel(plan, slots, known, me_ref, x_ref, e_ref, ge_ref, gk_ref, gv_ref,
                 core_ref, give_ref, keep_ref, ext_ref, wide_ref, abs_ref):
    extend(ext_ref, slot_cols(x_ref, slots) * slot_cols(e_ref, slots))
    m = split(ext_ref[...])
    for n, side in enumerate((gk_ref, gv_ref)):
        wide_ref[n, :, 0 : plan.width] = outer(m, split(side[...]))
    if known:
        wide_ref[2] = ge_ref[...]
    else:
        wide_ref[2, :, 0 : plan.width] = outer(m, split(slot_cols(ge_ref, slots)))
    tiles = []
    for r in range(plan.row_tiles):
        at = slice(r * ROWS, (r + 1) * ROWS)
        for n in range(3):
            tiles += [wide_ref[n, at, LANES * c : LANES * (c + 1)] for c in range(plan.wid_full)]
        tail = slice(LANES * plan.wid_full, LANES * (plan.wid_full + 1))
        tiles.append(joint_tail(wide_ref[0, at, tail], wide_ref[1, at, tail], plan.wid_tail))
        tiles.append(wide_ref[2, at, tail])
    deal(tiles, plan.leaf_tiles, abs_ref)
    me_graph, me_leaf = me_ref[0], me_ref[1]
    half = plan.graph_devices // 2
    for other in range(plan.leaf_devices):
        leaf = jnp.bitwise_xor(other, me_leaf)
        for r in range(plan.graph_devices):
            rel = distances(half)[r % half] + r // half
            source = abs_ref[jnp.bitwise_xor(rel, me_graph) * plan.leaf_devices + leaf]
            if other % 2:
                core_ref[other // 2, r] = source
            elif other // 2:
                give_ref[r] = source
            else:
                keep_ref[r] = source


def leaf_back_kernel(slots, layer, last, x_ref, e_ref, ge_ref, other_ref, gk_ref, gv_ref, square_ref,
                     new_gx_ref, new_ge_ref, flat_ref):
    gx_ref = other_ref
    sides = [gk_ref[...], gv_ref[...]] + ([slot_cols(ge_ref, slots)] if last else [])
    gm = 0.0 if last else other_ref[...]
    for n, side in enumerate(sides):
        gm += mul_pair(split(plain(square_ref[layer, :, n + 1, :], flat_ref)), split(side), NN)
    for s in range(slots):
        part = gm[:, LANES * s : LANES * (s + 1)]
        gx = part * e_ref[:, s, :]
        new_gx_ref[:, s, :] = gx_ref[:, s, :] + gx if last else gx
        new_ge_ref[:, s, :] = ge_ref[:, s, :] + part * x_ref[:, s, :]


def sixth_kernel(plan, slots, me_ref, g0, g1, g2, g3, res_ref, h2_ref, square_ref,
                 att_ref, h_ref, z_ref, unit1_ref, spread1_ref, unit2_ref, spread2_ref, top_ref, total_ref,
                 q_ref, k_ref, v_ref, s_ref, out_ref, in_ref, down_ref, bias_ref, gain_ref,
                 gq_ref, gk_ref, gv_ref, new_res_ref, keep_ref, give_ref, q_keep_ref, q_give_ref,
                 gatt_ref, p_ref, flat_ref, ext_ref, wide1_ref, wide2_ref, abs_ref, q_abs_ref):
    gq = tree([ref[...] for ref in (g0, g1, g2, g3)], jnp.add)
    grad = res_ref[...] + mul_narrow(split(plain(square_ref[1, :, 0, :], flat_ref)), split(gq), NN)
    query_gradient(plan, h2_ref[...], gq, me_ref[0], me_ref[1], ext_ref, wide1_ref, q_abs_ref, q_keep_ref, q_give_ref)
    gatt_ref[...], new_res_ref[...], g_f, dz, g_h1 = center_backward(
        grad, z_ref[...], unit1_ref[...], spread1_ref[...], unit2_ref[...], spread2_ref[...],
        out_ref, in_ref, down_ref, bias_ref, gain_ref, 0, flat_ref,
    )
    center_weights(
        plan, grad, att_ref[...], z_ref[...], unit1_ref[...], unit2_ref[...], new_res_ref[...], g_f, dz, g_h1,
        bias_ref, gain_ref, 0, me_ref[0], me_ref[1], ext_ref, wide1_ref, wide2_ref, abs_ref, keep_ref, give_ref,
    )
    attend_back(att_ref, gatt_ref, q_ref, k_ref, v_ref, s_ref, top_ref[...], total_ref[...], slots,
                None, p_ref, gq_ref, gk_ref, gv_ref)


def seventh_kernel(plan, me_ref, g0, g1, g2, g3, res_ref, h_ref, square_ref,
                   grad_ref, keep_ref, give_ref, flat_ref, ext_ref, wide_ref, abs_ref):
    gq = tree([ref[...] for ref in (g0, g1, g2, g3)], jnp.add)
    grad_ref[...] = res_ref[...] + mul_narrow(split(plain(square_ref[0, :, 0, :], flat_ref)), split(gq), NN)
    query_gradient(plan, h_ref[...], gq, me_ref[0], me_ref[1], ext_ref, wide_ref, abs_ref, keep_ref, give_ref)


def last_kernel(plan, routes, me_ref, *refs):
    count = len(routes)
    pieces, given, (hid_ref, bias_ref, gain_ref) = refs[:count], refs[count : count + 4], refs[count + 4 : count + 7]
    all_ref, square_ref, out_ref, in_ref, down_ref, sems = refs[count + 7 :]
    me_graph, me_leaf = me_ref[0], me_ref[1]
    width = plan.width
    for ref, (places, first, rows) in zip(pieces, routes):
        for n, (graph, leaf, core) in enumerate(places):
            owner = jnp.bitwise_xor(leaf, me_leaf)
            if core is not None:
                owner = owner // 2 * 2 + core
            all_ref[jnp.bitwise_xor(graph, me_graph), owner, first : first + rows, :] = ref[n]

    def tile(layer, kind, index):
        per = (plan.center_tiles, plan.query_tiles, plan.leaf_tiles)[kind]
        leaf, index = index if kind < 2 else (None, index)
        chunk, at = divmod(index, per)
        if kind == 2:
            chunk, leaf = divmod(chunk, plan.leaf_devices)
        at = (plan.bases[layer][kind] + at) * ROWS
        return all_ref[chunk, leaf, at : at + ROWS, :]

    hid_tail, wid_tail, full, wid = plan.hid_tail, plan.wid_tail, plan.hid_full, plan.wid_full

    def cut(c, whole, tail):
        size = LANES if c < whole else tail
        return slice(LANES * c, LANES * c + size), size

    def row_tile(r, layer):
        leaf, own = divmod(r, plan.share)
        rows = min(ROWS, width - r * ROWS)
        at = slice(r * ROWS, r * ROWS + rows)
        center = [tile(layer, 0, (leaf, own * plan.center_lanes + c)) for c in range(plan.center_lanes)]
        query = [tile(layer, 1, (leaf, own * plan.query_lanes + c)) for c in range(plan.query_lanes)]
        sides = [tile(layer, 2, r * plan.leaf_lanes + c) for c in range(plan.leaf_lanes)]
        tail = center[2 * full]
        ins = center[:full] + [tail]
        downs = center[full : 2 * full] + [pltpu.roll(tail, LANES - hid_tail, 1)]
        outs = center[2 * full + 1 :]
        joint = sides[3 * wid]
        keys = sides[:wid] + [joint]
        values = sides[wid : 2 * wid] + [pltpu.roll(joint, LANES - wid_tail, 1)]
        steps = sides[2 * wid : 3 * wid] + [sides[3 * wid + 1]]
        for c in range(full + 1):
            lanes, size = cut(c, full, hid_tail)
            in_ref[at, layer, lanes] = ins[c][:rows, :size]
            down_ref[at, layer, lanes] = downs[c][:rows, :size]
        for c in range(wid + 1):
            lanes, size = cut(c, wid, wid_tail)
            out_ref[at, layer, lanes] = outs[c][:rows, :size]
            for n, part in enumerate((query, keys, values, steps)):
                square_ref[layer, at, n, lanes] = part[c][:rows, :size]
        if r == width // ROWS:
            first = plan.last_row
            for c in range(full + 1):
                lanes, size = cut(c, full, hid_tail)
                hid_ref[layer : layer + 1, lanes] = ins[c][first : first + 1, :size]
            for c in range(wid + 1):
                lanes, size = cut(c, wid, wid_tail)
                found = ((query, 0), (outs, 0), (outs, 1), (outs, 3), (downs, 1), (values, 0), (steps, 0))
                for n, (part, row) in enumerate(found):
                    bias_ref[n, layer : layer + 1, lanes] = part[c][first + row : first + row + 1, :size]
                gain_ref[layer, 0:1, lanes] = outs[c][first + 2 : first + 3, :size]
                gain_ref[layer, 1:2, lanes] = downs[c][first + 2 : first + 3, :size]

    copies = []
    for block in range(plan.blocks):
        tiles = range(block * plan.row_tiles // plan.blocks, (block + 1) * plan.row_tiles // plan.blocks)
        for r in tiles:
            for layer in range(LAYERS):
                row_tile(r, layer)
        at = pl.ds(tiles.start * ROWS, min(tiles.stop * ROWS, width) - tiles.start * ROWS)
        for n, (here, there) in enumerate(zip((square_ref, out_ref, in_ref, down_ref), given)):
            if n:
                here, there = here.at[at], there.at[at]
            else:
                here, there = here.at[:, at], there.at[:, at]
            copies.append(pltpu.make_async_copy(here, there, sems.at[block, n]))
            copies[-1].start()
    for copy in copies:
        copy.wait()


def after(value, *others):
    return lax.optimization_barrier((value, *others))[0]


def swap(values, axis, size, distance):
    pairs = [(i, i ^ distance) for i in range(size)]
    return jax.tree.map(lambda v: lax.ppermute(v, axis, pairs), values)


def distances(count):
    bits = count.bit_length() - 1
    return [2 * sum(((n >> b) & 1) << (bits - 1 - b) for b in range(bits)) for n in range(count)]


class Clock:
    def __init__(self):
        self.last = ()

    def wait(self, value):
        value = after(value, *self.last)
        self.last = (value,)
        return value

    def mark(self, *values):
        self.last = values


class Stream:
    def __init__(self, chain):
        self.chain, self.result, self.alive = chain, None, True
        self.step()

    def step(self):
        if self.alive:
            try:
                next(self.chain)
            except StopIteration as end:
                self.alive, self.result = False, end.value

    def finish(self):
        while self.alive:
            self.step()
        return self.result


def graph_scatter(clock, keep, give, size):
    own, got = keep, swap(give, "graphs", size, 1)
    distance = 2
    while distance < size:
        yield
        got = clock.wait(got)
        if 2 * distance < size:
            half = own.shape[0] // 2
            far = own[half:] + got[half:]
            own = own[:half] + got[:half]
        else:
            own = own + got
            far = jnp.concatenate([own[1:], own[:1]], axis=0)
        clock.mark(far)
        got = swap(far, "graphs", size, distance)
        distance *= 2
    return own, got


def side_scatter(clock, core, give, keep, queries, sizes):
    got = swap(core, "leaves", sizes[1], 1)
    yield
    got = clock.wait(got)
    far = give + got[1]
    own = keep + got[0]
    clock.mark(far)
    far = swap(far, "leaves", sizes[1], 2)
    yield
    far = clock.wait(far)
    half = own.shape[0] // 2
    q_keep, q_give = queries()
    q_give = jnp.concatenate([q_give, own[half:] + far[half:]], axis=1)
    clock.mark(q_give)
    chain = graph_scatter(
        clock, jnp.concatenate([q_keep, own[:half] + far[:half]], axis=1), q_give, sizes[0]
    )
    return (yield from chain)


class Spread:
    def __init__(self, clock, block, turns, sizes, first, early):
        self.clock, self.sizes, self.first, self.early = clock, sizes, first, early
        self.block, self.turns = block, turns
        self.places = [(0, 0), (sizes[0] // 2, 0)]
        self.near = self.far = None
        self.send()

    def send(self):
        turn = self.turns[0]
        if turn:
            self.got = swap(self.block, "graphs", self.sizes[0], turn)
            self.there = [(g ^ turn, f) for g, f in self.places]
        else:
            self.got = swap(self.block, "leaves", self.sizes[1], 2)
            self.there = [(g, f ^ 2) for g, f in self.places]
        if self.early and len(self.turns) == 1:
            self.give_near = swap(self.block, "leaves", self.sizes[1], 1)

    def step(self):
        if not self.turns:
            return
        got = self.clock.wait(self.got)
        self.turns = self.turns[1:]
        if self.turns:
            self.block = jnp.concatenate([self.block, got], axis=0)
            self.places = self.places + self.there
            self.clock.mark(self.block)
            self.send()
        else:
            self.got = got
            self.give_far = swap(got, "leaves", self.sizes[1], 1)

    def take_near(self):
        while len(self.turns) > 1:
            self.step()
        pairs = [[n, n + 1] for n in range(0, self.sizes[1], 2)]
        self.near = self.clock.wait(
            lax.all_gather(after(self.block, *self.clock.last), "leaves", axis_index_groups=pairs)
        )

    def take_far(self):
        while self.turns:
            self.step()
        self.far = self.clock.wait(self.give_far)

    def pieces(self):
        while self.turns:
            self.step()
        far = self.give_far if self.far is None else self.far
        found = [
            (self.got, [(g, f, None) for g, f in self.there]),
            (far, [(g, f ^ 1, None) for g, f in self.there]),
        ]
        if self.near is None:
            found.append((self.block, [(g, f, None) for g, f in self.places]))
            found.append((self.give_near, [(g, f ^ 1, None) for g, f in self.places]))
        else:
            joined = self.near.reshape(-1, *self.near.shape[2:])
            found.append((joined, [(g, f, core) for core in range(2) for g, f in self.places]))
        return [(v, tuple(at), self.first) for v, at in found]


def gather(clock, sums, turns, sizes, first, early, late):
    totals = [own + clock.wait(got) for own, got in sums]
    if len(totals) == 1 or totals[0].shape != totals[1].shape:
        total = jnp.concatenate(totals, axis=1)
        middle = total.shape[1] // 2 // ROWS * ROWS
        totals = [total[:, :middle], total[:, middle:]]
    clock.mark(*totals)
    ways = {"x": [0], "y": [1], "z": [1 << n for n in range(1, sizes[0].bit_length() - 2)]}
    chains = []
    for block, order in zip(totals, (turns, turns.translate(str.maketrans("xy", "yx")))):
        chains.append((block, [way for turn in order for way in ways[turn]], sizes, first, early))
        first += block.shape[1]
    (block, *rest), later = chains
    run = Spread(clock, block, *rest)
    if late:
        return run, lambda: Spread(clock, after(later[0], *clock.last), *later[1:])
    return run, Spread(clock, *later)


def on_device(
    sizes,
    centers,
    leaf_nodes,
    edges,
    leaf_counts,
    square,
    out_proj,
    ff_in,
    ff_out,
    ff_bias,
    biases,
    gains,
    cot_center,
    cot_edges,
):
    graphs, slots, width = leaf_nodes.shape
    hidden = ff_in.shape[2]
    graph_devices, leaf_devices = sizes
    plan = Plan(width, hidden, graph_devices, leaf_devices)
    me = jnp.stack([lax.axis_index("graphs"), lax.axis_index("leaves")]).astype(jnp.int32)

    h = centers.T
    x = leaf_nodes.transpose(2, 1, 0)
    e = edges.transpose(2, 1, 0)
    count = leaf_counts.reshape(1, graphs)
    sq = square.transpose(0, 2, 1, 3)
    wo = out_proj.transpose(1, 0, 2)
    w1 = ff_in.transpose(1, 0, 2)
    w2 = ff_out.transpose(2, 0, 1)
    bias = biases.transpose(1, 0, 2)
    gc = cot_center.T
    ge = cot_edges.transpose(2, 1, 0)

    base = ceil_div(width, ROWS) * ROWS
    wide = plan.share_rows
    lanes = ceil_div(hidden, LANES) * LANES
    shape = lambda *s: jax.ShapeDtypeStruct(s, F32)
    scratch = lambda *s: pltpu.VMEM(s, F32)
    cell = (width, graphs)
    row = (1, graphs)
    flat = (width, lanes)
    sides = (width, slots * graphs)
    cube = (width, slots, graphs)
    heads = (HEAD_ROWS, graphs)
    scores = (slots, HEAD_ROWS, graphs)
    part = (base + 2 * HEAD_ROWS, graphs)
    half = graph_devices // 2

    def call(kernel, ins, outs, scratches, took, first_smem=True):
        return pl.pallas_call(
            kernel,
            in_specs=[SMEM if first_smem and n == 0 else VMEM for n in range(len(ins))],
            out_specs=[VMEM] * len(outs),
            out_shape=[shape(*s) for s in outs],
            scratch_shapes=[scratch(*s) for s in scratches],
            compiler_params=pltpu.CompilerParams(vmem_limit_bytes=KERNEL_VMEM),
            cost_estimate=pl.CostEstimate(flops=int(took * FLOPS_A_US), bytes_accessed=0, transcendentals=0),
        )(*ins)

    def around(value):
        return swap(value, "leaves", leaf_devices, 1), swap(value, "leaves", leaf_devices, 2)

    def all_around(value, near, far):
        return value, near, far, swap(far, "leaves", leaf_devices, 1)

    firsts = (part, cell, sides, sides, scores, cube)
    near_shapes = (cube, cube, cell, (1, width, 4, width), bias.shape)
    part1, q1, k1, v1, s1, e1 = pl.pallas_call(
        functools.partial(first_kernel, slots),
        in_specs=[SMEM] + [HBM] * 6,
        out_specs=[VMEM] * len(firsts),
        out_shape=[shape(*s) for s in firsts],
        scratch_shapes=[
            pltpu.VMEM(count.shape, jnp.int32),
            *[scratch(*s) for s in near_shapes],
            scratch(*scores),
            pltpu.SemaphoreType.DMA((6,)),
        ],
        compiler_params=pltpu.CompilerParams(vmem_limit_bytes=KERNEL_VMEM),
        cost_estimate=pl.CostEstimate(flops=int(5 * FLOPS_A_US), bytes_accessed=0, transcendentals=0),
    )(me, *[pltpu.with_memory_space_constraint(v, pltpu.HBM) for v in (count, x, e, h, sq, bias)])
    near, far = around(part1)
    k2, v2, e2 = call(
        functools.partial(second_kernel, slots), (x, e1, sq, bias), (sides, sides, cube), (), 5, first_smem=False
    )
    parts1 = all_around(part1, near, after(far, k2))
    part2, att1, top1, total1, unit1, spread1, z1, unit2, spread2, h2, q2, s2 = call(
        functools.partial(third_kernel, slots),
        (me, count, *parts1, h, k2, v2, sq, wo, w1, w2, ff_bias, bias, gains),
        (part, cell, heads, heads, cell, row, (hidden, graphs), cell, row, cell, cell, scores),
        ((leaf_devices, *heads), scores, flat),
        8,
    )
    near, far = around(part2)
    side_rows = plan.row_tiles * ROWS
    side_lanes = ceil_div(width, LANES) * LANES
    edge_step, edge_weight = call(
        functools.partial(edge_kernel, slots, 1),
        (x, e1, after(ge, part2), sq),
        (sides, (side_rows, side_lanes)),
        (flat, (side_rows, slots * graphs)),
        3,
        first_smem=False,
    )
    parts2 = all_around(part2, near, after(far, edge_step))
    center_chunk = (half, plan.center_tiles * ROWS, LANES)
    query_chunk = (half, plan.query_tiles * ROWS, LANES)
    leaf_chunk = (graph_devices, plan.leaf_tiles * ROWS, LANES)
    ext = (wide * leaf_devices, graphs)
    tall = (hidden, graphs)
    center_out, gq2, gk2, gv2, res2, att2, z2, unit1b, unit2b, gf2, dz2, gh12 = call(
        functools.partial(fourth_kernel, slots),
        (*parts2, h2, q2, k2, v2, s2, gc, wo, w1, w2, ff_bias, bias, gains),
        (cell, cell, sides, sides, cell, cell, tall, cell, cell, cell, tall, cell),
        ((leaf_devices, *heads), heads, heads, cell, scores, flat),
        10,
        first_smem=False,
    )
    clock = Clock()
    side_scratch = (
        (plan.row_tiles * ROWS, slots * graphs),
        (3, plan.row_tiles * ROWS, ceil_div(width, LANES) * LANES),
        (graph_devices * leaf_devices, *leaf_chunk[1:]),
    )
    side_shapes = ((2, *leaf_chunk), leaf_chunk, leaf_chunk)

    near, far = around(gq2)
    keep2, give2 = call(
        functools.partial(weights_kernel, plan),
        (me, gc, att2, z2, unit1b, unit2b, res2, gf2, dz2, gh12, bias, gains),
        (center_chunk, center_chunk),
        (ext, (wide, lanes), (wide, lanes), (graph_devices, *center_chunk[1:])),
        3,
    )
    center2 = Stream(graph_scatter(clock, keep2, give2, graph_devices))
    far = after(far, keep2)
    gqs2 = all_around(gq2, near, far)
    core2, lgive2, lkeep2 = call(
        functools.partial(fifth_kernel, plan, slots, True),
        (me, x, e1, edge_weight, after(gk2, far), gv2),
        side_shapes,
        side_scratch,
        4,
    )
    side2 = Stream(side_scatter(clock, core2, lgive2, lkeep2, lambda: (qkeep2, qgive2), sizes))
    gqs2 = (after(gqs2[0], core2), *gqs2[1:])
    gq1, gk1, gv1, res1, keep1, give1, qkeep2, qgive2 = call(
        functools.partial(sixth_kernel, plan, slots),
        (me, *gqs2, res2, h2, sq, att1, h, z1, unit1, spread1, unit2, spread2, top1, total1,
         q1, k1, v1, s1, wo, w1, w2, bias, gains),
        (cell, sides, sides, cell, center_chunk, center_chunk, query_chunk, query_chunk),
        (cell, scores, flat, ext, (wide, lanes), (wide, lanes),
         (graph_devices, *center_chunk[1:]), (graph_devices, *query_chunk[1:])),
        6,
    )
    near, far = around(gq1)
    center1 = Stream(graph_scatter(clock, keep1, give1, graph_devices))
    clock.mark(gq1)
    done = {}

    def upper_messages():
        done["upper"] = call(
            functools.partial(leaf_back_kernel, slots, 1, False),
            (x, e1, ge, edge_step, after(gk2, *clock.last), gv2, sq),
            (cube, cube),
            (flat,),
            0.4,
            first_smem=False,
        )
        clock.mark(done["upper"][1])

    def leaf_weights():
        sent = call(
            functools.partial(fifth_kernel, plan, slots, False),
            (me, x, e, done["upper"][1], after(gk1, *clock.last), gv1),
            side_shapes,
            side_scratch,
            0.4,
        )
        clock.mark(sent[0])
        streams["S1"] = Stream(side_scatter(clock, *sent, lambda: done["queries"], sizes))

    def leaf_messages():
        done["leaf"] = call(
            functools.partial(leaf_back_kernel, slots, 0, True),
            (x, e, done["upper"][1], done["upper"][0], after(gk1, *clock.last), gv1, sq),
            (cube, cube),
            (flat,),
            0.3,
            first_smem=False,
        )
        clock.mark(done["leaf"][0])

    def query_near():
        done["near"] = clock.wait(near)

    def query_far():
        done["far"] = clock.wait(far)
        done["hop"] = swap(done["far"], "leaves", leaf_devices, 1)

    def query_weights():
        hop = clock.wait(done["hop"])
        arrived = done.get("near", near)
        done["center"], *done["queries"] = call(
            functools.partial(seventh_kernel, plan),
            (me, gq1, arrived, done["far"], hop, res1, h, sq),
            (cell, query_chunk, query_chunk),
            (flat, ext, (wide, lanes), (graph_devices, *query_chunk[1:])),
            0.2,
        )
        clock.mark(done["center"])

    streams = {"C2": center2, "C1": center1, "S2": side2}
    kernels = {
        "upper_messages": upper_messages,
        "leaf_weights": leaf_weights,
        "leaf_messages": leaf_messages,
        "query_near": query_near,
        "query_far": query_far,
        "query_weights": query_weights,
    }
    groups = {"c2": ("C2",), "c1": ("C1",), "cs": ("C1", "S2"), "s": ("S2", "S1"), "s2": ("S2",), "s1": ("S1",)}
    firsts = {"C2": 0, "C1": plan.center_tiles, "S2": 2 * plan.center_tiles}
    firsts["S1"] = firsts["S2"] + plan.side_tiles
    for step in ORDER:
        name, mark = step.rstrip("<!"), step[len(step.rstrip("<!")) :]
        if name in kernels:
            kernels[name]()
        elif name in groups:
            parts = groups[name]
            streams[name + "a"], streams[name + "b"] = gather(
                clock,
                [streams[part].finish() for part in parts],
                TURNS[name],
                sizes,
                firsts[parts[0]] * ROWS,
                name + "a<" not in ORDER,
                name + "b!" in ORDER,
            )
        elif mark == "!":
            streams[name] = streams[name]()
        else:
            getattr(streams[name], {"": "step", "<": "take_near", "<<": "take_far"}[mark])()
    (gx1, ge0), grad_center = done["leaf"], done["center"]
    pieces, routes = [], []
    for name in (group + half for group in TURNS for half in "ab"):
        for piece, places, first in streams[name].pieces():
            pieces.append(piece)
            routes.append((places, first, piece.shape[1]))
    large = ((LAYERS, width, 4, width), (width, LAYERS, width), (width, LAYERS, hidden), (width, LAYERS, hidden))
    small = ((LAYERS, hidden), (7, LAYERS, width), (LAYERS, 2, width))
    g_square, g_out, g_in, g_down, g_hid, g_bias, g_gain = pl.pallas_call(
        functools.partial(last_kernel, plan, routes),
        in_specs=[SMEM] + [VMEM] * len(pieces),
        out_specs=[HBM] * len(large) + [VMEM] * len(small),
        out_shape=[shape(*s) for s in large + small],
        scratch_shapes=[
            scratch(graph_devices, leaf_devices, plan.all_tiles * ROWS, LANES),
            *[scratch(*s) for s in large],
            pltpu.SemaphoreType.DMA((plan.blocks, len(large))),
        ],
        compiler_params=pltpu.CompilerParams(vmem_limit_bytes=LAST_VMEM),
    )(me, *pieces)
    return (
        center_out.T,
        e2.transpose(2, 1, 0),
        grad_center.T,
        gx1.transpose(2, 1, 0),
        ge0.transpose(2, 1, 0),
        g_square.transpose(0, 2, 1, 3),
        g_out.transpose(1, 0, 2),
        g_in.transpose(1, 0, 2),
        g_down.transpose(1, 2, 0),
        g_hid,
        g_bias.transpose(1, 0, 2),
        g_gain,
    )


def solution(mesh):
    sizes = (mesh.shape["graphs"], mesh.shape["leaves"])
    in_specs = (
        P("graphs", None),
        P("graphs", "leaves", None),
        P("graphs", "leaves", None),
        P("graphs"),
        P(),
        P(),
        P(),
        P(),
        P(),
        P(),
        P(),
        P("graphs", None),
        P("graphs", "leaves", None),
    )
    out_specs = (
        P("graphs", None),
        P("graphs", "leaves", None),
        P("graphs", None),
        P("graphs", "leaves", None),
        P("graphs", "leaves", None),
        P(),
        P(),
        P(),
        P(),
        P(),
        P(),
        P(),
    )
    return jax.shard_map(
        functools.partial(on_device, sizes),
        mesh=mesh,
        in_specs=in_specs,
        out_specs=out_specs,
        check_vma=False,
    )
```
